256 devices in a mesh: view: 16 (over z, core), span: 16 (over x, y).
Axes of the slice: x: 4, y: 4, z: 8, core: 2. Of those that a mesh axis runs over, the one named last changes fastest.
Arguments:
- tokens: bfloat16 [16, 4096, 1024], P('view', 'span'), may hold values from -6 to 6
- scan_order: int32 [16, 4096], P('view'), may hold values from 0 to 4095, as said below
- w_merge: bfloat16 [4096, 1024], replicated, may hold values from -0.09375 to 0.09375
- bias: bfloat16 [1024], replicated, may hold values from -4 to 4
- cotangent: bfloat16 [16, 1024, 1024], P('view', 'span'), may hold values from -6 to 6
Outputs:
- merged_out: bfloat16 [16, 1024, 1024], P('view', 'span')
- token_grad: bfloat16 [16, 4096, 1024], P('view', 'span')
- weight_grad: float32 [4096, 1024], P(('view', 'span'))
- bias_grad: float32 [1024], replicated
The draws below stay inside these ranges and needn't reach their ends.
Inputs may be any that keep to these rules, and one draw needn't show every extreme that they name: `scan_order`: each row is a permutation of the raster indices of one view. Call tokens 256 * b to 256 * (b + 1) - 1 band b, and scan positions 256 * c to 256 * (c + 1) - 1 block c: every block holds at most 24 tokens of any band, and in every row each block holds exactly 24 tokens of some band.
All inputs are finite; a program needn't handle non-finite values.
Results may differ from the reference program's by a relative error of at most 0.001.
Values may be sent and summed in bfloat16 or wider, within the bound.
A program may use at most 128 MiB of HBM per device.

```python
import math
import jax
import jax.numpy as jnp
from jax import lax

DM = 1024
DO = 1024
MERGE_IN = 4096
COLS = 128
VIEWS = 16
ROWS = 32
TOK_DEV = 256
TOK_VIEW = 4096
MTOK_VIEW = 1024
N_SPAN = 16


def scan_one_view(key):
    spans = N_SPAN
    base = TOK_DEV // spans
    half = base // 2
    key_a, key_b, key_c, key_d = jax.random.split(key, 4)
    first = jax.random.permutation(key_a, spans)
    offset = jax.random.randint(key_b, (), 1, spans)
    second = (first + offset) % spans
    owner_ids = jnp.arange(spans, dtype=jnp.int32)
    counts = base + half * (owner_ids[None, :] == first[:, None]).astype(jnp.int32) - half * (owner_ids[None, :] == second[:, None]).astype(jnp.int32)
    column_end = jnp.cumsum(counts, axis=0)
    column_start = column_end - counts
    row_start = jnp.cumsum(counts, axis=1) - counts
    ranks = jnp.arange(TOK_DEV, dtype=jnp.int32)
    span_of = jnp.sum((column_end.T[:, None, :] <= ranks[None, :, None]).astype(jnp.int32), axis=2)
    owner_grid = jnp.broadcast_to(owner_ids[:, None], (spans, TOK_DEV))
    within = row_start[span_of, owner_grid] + ranks[None, :] - column_start[span_of, owner_grid]
    shuffles = jax.vmap(lambda k: jax.random.permutation(k, TOK_DEV))(jax.random.split(key_c, spans))
    positions = span_of * TOK_DEV + shuffles[span_of, within]
    band_shuffle = jax.vmap(lambda k: jax.random.permutation(k, TOK_DEV))(jax.random.split(key_d, spans))
    token_ids = owner_grid * TOK_DEV + band_shuffle
    order = jnp.zeros((TOK_VIEW,), jnp.int32).at[positions.reshape(-1)].set(token_ids.reshape(-1).astype(jnp.int32))
    return order


def draw_scan_order(key, part):
    keys = jax.random.split(jax.random.fold_in(key, 7), VIEWS)
    return jax.vmap(scan_one_view)(keys).astype(jnp.int32)


def with_spikes(drawn, key, source, target, shards_of, factor):
    def block_of(axis_at):
        return (jnp.arange(drawn.shape[axis_at]) // (drawn.shape[axis_at] // shards_of)).reshape((-1,) + (1,) * (drawn.ndim - 1 - axis_at))

    near = jax.random.permutation(key, shards_of)[block_of(target)]
    other_side = (block_of(target) + shards_of // 2) % shards_of
    return jnp.where((block_of(source) == near) | (block_of(source) == other_side), factor * drawn, drawn)


def block_scale(stream_key, dims, cuts, smallest, top_value):
    factor_of, own = 1.0, jax.random.fold_in(stream_key, 6)
    for position, parts in cuts:
        heights = jnp.exp(jax.random.uniform(jax.random.fold_in(own, position), (parts,), jnp.float32, smallest / len(cuts), top_value / len(cuts)))
        factor_of = factor_of * jnp.repeat(heights, dims[position] // parts).reshape([-1 if axis == position else 1 for axis in range(len(dims))])
    return factor_of


def bell_draw(stream_key, extent, spread, reach, cuts=(), kind=jnp.bfloat16):
    entries = spread * jax.random.normal(stream_key, extent, jnp.float32)
    if cuts:
        entries = entries * block_scale(stream_key, extent, cuts, -0.22, 0.18)
    return jnp.clip(entries, -reach, reach).astype(kind)


def bell_draw_with(rng, shape, width, bound, shards, heavy, kind=jnp.bfloat16):
    entries = width * jax.random.normal(rng, shape, jnp.float32)
    if shards:
        entries = entries * block_scale(rng, shape, shards, -0.22, 0.18)
    return jnp.clip(with_spikes(entries, jax.random.fold_in(rng, 3), *heavy), -bound, bound).astype(kind)


def setup_inputs(seed: int = 0) -> dict:
    key_of = jax.random.split(jax.random.key(seed), 6)
    tokens = bell_draw_with(key_of[0], (VIEWS, TOK_VIEW, DM), 1.0, 6.0, ((0, 16), (1, 16)), (1, 2, 16, 2.0))
    scan_order = draw_scan_order(jax.random.fold_in(key_of[5], 71), 0)
    w_merge = bell_draw(key_of[2], (MERGE_IN, DO), MERGE_IN ** -0.5, 0.09375)
    bias = bell_draw(key_of[3], (DO,), 1.0, 4.0)
    cotangent = bell_draw(key_of[4], (VIEWS, MTOK_VIEW, DO), 1.0, 6.0, ((0, 16), (1, 16)))
    return dict(tokens=tokens, scan_order=scan_order, w_merge=w_merge, bias=bias, cotangent=cotangent)


def one_view(w_merge, bias, order, feats, grads):
    raster = jnp.zeros((TOK_VIEW, DM), jnp.bfloat16).at[order].set(feats)
    merged = raster.reshape(ROWS // 2, 2, COLS // 2, 2, DM).transpose(0, 2, 1, 3, 4).reshape(MTOK_VIEW, MERGE_IN)
    merged_out = (jnp.dot(merged, w_merge, preferred_element_type=jnp.float32) + bias.astype(jnp.float32)).astype(jnp.bfloat16)
    grad_merged = lax.dot_general(grads, w_merge, (((1,), (1,)), ((), ())), preferred_element_type=jnp.float32).astype(jnp.bfloat16)
    grad_raster = grad_merged.reshape(ROWS // 2, COLS // 2, 2, 2, DM).transpose(0, 2, 1, 3, 4).reshape(TOK_VIEW, DM)
    token_grad = grad_raster[order]
    weight_part = lax.dot_general(merged, grads, (((0,), (0,)), ((), ())), preferred_element_type=jnp.float32)
    return (merged_out, token_grad, weight_part)

def reference(tokens, scan_order, w_merge, bias, cotangent):

    def step(carry, items):
        order, feats, grads = items
        merged_out, token_grad, weight_part = one_view(w_merge, bias, order, feats, grads)
        return (carry + weight_part, (merged_out, token_grad))
    start = jnp.zeros((MERGE_IN, DO), jnp.float32)
    weight_sum, stacked = lax.scan(step, start, (scan_order, tokens, cotangent))
    scale = 1.0 / math.sqrt(VIEWS * MTOK_VIEW)
    bias_grad = lax.optimization_barrier(jnp.sum(cotangent.astype(jnp.float32), axis=(0, 1))) * scale
    return (stacked[0], stacked[1], weight_sum * scale, bias_grad)
```

```python
import functools
import math

import jax
import jax.numpy as jnp
from jax import lax
from jax.experimental import pallas as pl
from jax.experimental.pallas import tpu as pltpu
from jax.sharding import PartitionSpec as P

MESH = pl.DeviceIdType.MESH
F32 = jnp.float32
BF16 = jnp.bfloat16
NN = (((1,), (0,)), ((), ()))
NT = (((1,), (1,)), ((), ()))
TN = (((0,), (0,)), ((), ()))


def dot(a, b, dims=NN):
    return lax.dot_general(a, b, dims, preferred_element_type=F32)


def one_hot(hit):
    return jnp.where(hit, 1.0, 0.0).astype(BF16)


def kernel(
    views,
    spans,
    cols,
    scale,
    tokens_ref,
    order_ref,
    w_hbm,
    bias_ref,
    cot_ref,
    merged_out_ref,
    token_grad_ref,
    weight_grad_ref,
    bias_grad_ref,
    w_ref,
    out_ref,
    recv_ref,
    back_ref,
    ret_ref,
    pick_ref,
    place_ref,
    rank_ref,
    code_ref,
    merged_ref,
    grad_ref,
    blocks_ref,
    cot_a,
    cot_b,
    half_send,
    half_own,
    half_recv,
    final_ref,
    view_bias,
    w_sem,
    tok_send,
    tok_recv,
    back_send,
    back_recv,
    blk_send,
    blk_recv,
    one_send,
    one_recv,
    two_send,
    two_recv,
    bias_send,
    bias_recv,
    pair_send,
    pair_recv,
    fin_send,
    fin_recv,
):
    v = lax.axis_index("view")
    s = lax.axis_index("span")
    core = lax.rem(v, 2)
    z = v // 2
    side = 4
    x, y = s // side, lax.rem(s, side)
    tok = tokens_ref.shape[1]
    dm = tokens_ref.shape[2]
    half = dm // 2
    mt = tok // 4
    cap = 3 * (tok // spans) // 2
    slot = 2 * cap
    nz = views // 2
    part = final_ref.shape[1]
    width = blocks_ref.shape[2]
    hw = width // 2

    t_in = lax.rem(v * spans + s, views)
    own_span = (v * spans + s) // views
    own_core = t_in // nz

    def source(k):
        return k * 2 + own_core, own_span

    def target(j):
        r = s * views + core * nz + j
        return r // spans, lax.rem(r, spans)

    barrier = pltpu.get_barrier_semaphore()

    @pl.loop(1, spans)
    def _(i):
        pl.semaphore_signal(barrier, inc=1, device_id=(v, s ^ i), device_id_type=MESH)

    @pl.loop(1, views)
    def _(i):
        pl.semaphore_signal(barrier, inc=1, device_id=(v ^ i, s), device_id_type=MESH)

    @pl.loop(0, nz)
    def _(k):
        tv, ts = source(k)

        @pl.when(jnp.logical_or(tv != v, ts != s))
        def _():
            pl.semaphore_signal(barrier, inc=1, device_id=(tv, ts), device_id_type=MESH)

    w_copy = pltpu.make_async_copy(w_hbm, w_ref, w_sem)
    w_copy.start()

    before = one_hot(
        lax.broadcasted_iota(jnp.int32, (tok, tok), 0)
        < lax.broadcasted_iota(jnp.int32, (tok, tok), 1)
    )
    mine = order_ref[0:1, pl.ds(pl.multiple_of(s * tok, tok), tok)]
    owner = lax.shift_right_logical(mine, int(math.log2(tok)))
    hot = jnp.where(lax.broadcasted_iota(jnp.int32, (spans, tok), 0) == owner, 1.0, 0.0)
    rank = jnp.sum(dot(hot.astype(BF16), before) * hot, axis=0, keepdims=True).astype(jnp.int32)
    first = owner * slot + rank
    slots = jnp.concatenate([first, first + cap], axis=1)

    cot = cot_ref[0]
    cot_a[x, y] = cot[:, :half]
    cot_b[x, y] = cot[:, half:]

    group = spans // 4

    @pl.loop(0, 4)
    def _(t):
        rows = group * slot
        pick = one_hot(lax.broadcasted_iota(jnp.int32, (rows, 2 * tok), 0) + t * rows == slots)
        pick_ref[pl.ds(pl.multiple_of(t * rows, rows), rows), :] = pick
        sent = dot(pick[:, :tok], tokens_ref[0, :, :half]) + dot(
            pick[:, tok:], tokens_ref[0, :, half:]
        )
        out_ref[pl.ds(t * group, group)] = sent.astype(BF16).reshape(group, slot, half)

    recv_ref[s] = out_ref[s]

    waits = (spans - 1) + (views - 1) + nz
    same = jnp.logical_and(own_span == s, own_core == core)
    pl.semaphore_wait(barrier, jnp.where(same, waits - 1, waits))

    def swap(src, dst, send, recv, i):
        return pltpu.make_async_remote_copy(
            src_ref=src,
            dst_ref=dst,
            send_sem=send.at[i],
            recv_sem=recv.at[i],
            device_id=(v, s ^ i),
            device_id_type=MESH,
        )

    def tok_copy(i):
        return swap(out_ref.at[s ^ i], recv_ref.at[s], tok_send, tok_recv, i)

    def back_copy(i):
        return swap(back_ref.at[s ^ i], ret_ref.at[s], back_send, back_recv, i)

    def blk_copy(i):
        d = s ^ i
        src = merged_ref.at[:, pl.ds(pl.multiple_of(d * width, width), width)]
        return swap(src, blocks_ref.at[s], blk_send, blk_recv, i)

    def one_y(i):
        return pltpu.make_async_remote_copy(
            src_ref=cot_a.at[x, y],
            dst_ref=cot_a.at[x, y],
            send_sem=one_send.at[i],
            recv_sem=one_recv.at[i],
            device_id=(v, s ^ i),
            device_id_type=MESH,
        )

    def one_x(i):
        return pltpu.make_async_remote_copy(
            src_ref=cot_b.at[x, y],
            dst_ref=cot_b.at[x, y],
            send_sem=one_send.at[side + i],
            recv_sem=one_recv.at[side + i],
            device_id=(v, s ^ (i * side)),
            device_id_type=MESH,
        )

    def two_x(i):
        return pltpu.make_async_remote_copy(
            src_ref=cot_a.at[x],
            dst_ref=cot_a.at[x],
            send_sem=two_send.at[i],
            recv_sem=two_recv.at[i],
            device_id=(v, s ^ (i * side)),
            device_id_type=MESH,
        )

    def two_y(i):
        return pltpu.make_async_remote_copy(
            src_ref=cot_b.at[:, y],
            dst_ref=cot_b.at[:, y],
            send_sem=two_send.at[side + i],
            recv_sem=two_recv.at[side + i],
            device_id=(v, s ^ i),
            device_id_type=MESH,
        )

    def bias_copy(i):
        return pltpu.make_async_remote_copy(
            src_ref=view_bias.at[v],
            dst_ref=view_bias.at[v],
            send_sem=bias_send.at[i],
            recv_sem=bias_recv.at[i],
            device_id=(v ^ i, s),
            device_id_type=MESH,
        )

    pair = pltpu.make_async_remote_copy(
        src_ref=half_send,
        dst_ref=half_recv,
        send_sem=pair_send.at[0],
        recv_sem=pair_recv.at[0],
        device_id=(v ^ 1, s),
        device_id_type=MESH,
    )

    def fin_copy(j):
        tv, ts = target(j)
        return pltpu.make_async_remote_copy(
            src_ref=half_own.at[pl.ds(pl.multiple_of(j * part, part), part), :],
            dst_ref=final_ref.at[z],
            send_sem=fin_send.at[j],
            recv_sem=fin_recv.at[z],
            device_id=(tv, ts),
            device_id_type=MESH,
        )

    def fin_arrival(k):
        return pltpu.make_async_remote_copy(
            src_ref=half_own.at[pl.ds(0, part), :],
            dst_ref=final_ref.at[k],
            send_sem=fin_send.at[0],
            recv_sem=fin_recv.at[k],
            device_id=(v ^ 1, s),
            device_id_type=MESH,
        )

    @pl.loop(1, spans)
    def _(i):
        tok_copy(i).start()

    @pl.loop(1, side)
    def _(i):
        one_y(i).start()
        one_x(i).start()

    order = jnp.concatenate([order_ref[0:1, c * tok : (c + 1) * tok] for c in range(spans)], axis=0)
    arriving = lax.shift_right_logical(order, int(math.log2(tok))) == s
    arrive = jnp.where(arriving, 1.0, 0.0)
    rank_in = dot(arrive.astype(BF16), before)
    rank_ref[...] = jnp.where(arriving, rank_in, -1.0)
    local = lax.rem(order, tok)
    col = lax.rem(local, cols)
    quadrant = (local // cols) * 2 + lax.rem(col, 2)
    code_ref[...] = jnp.where(arriving, quadrant * mt + col // 2 + 1, 0).astype(F32)

    @pl.loop(0, spans)
    def _(c):
        rk = rank_ref[pl.ds(c, 1), :]
        cd = code_ref[pl.ds(c, 1), :]
        row = lax.broadcasted_iota(jnp.int32, (slot, tok), 0)
        k = jnp.where(row >= cap, row - cap, row).astype(F32)
        to = jnp.sum(jnp.where(rk == k, cd, 0.0), axis=1, keepdims=True).astype(jnp.int32)
        row = lax.broadcasted_iota(jnp.int32, (slot, 2 * tok), 0)
        lane = lax.broadcasted_iota(jnp.int32, (slot, 2 * tok), 1)
        wanted = jnp.where(row >= cap, lane - tok, lane) + 1
        wanted = jnp.where(wanted > tok, 0, wanted)
        place_ref[pl.ds(pl.multiple_of(c * slot, slot), slot), :] = one_hot(
            jnp.logical_and(to == wanted, wanted > 0)
        )

    @pl.loop(1, side)
    def _(i):
        one_y(i).wait_recv()
        one_x(i).wait_recv()

    @pl.loop(1, side)
    def _(i):
        two_x(i).start()
        two_y(i).start()

    w_copy.wait()

    @pl.loop(0, 8)
    def _(t):
        q, h = t // 2, lax.rem(t, 2)
        rows = w_ref[pl.ds(pl.multiple_of(t * half, half), half), :]
        g = dot(cot_ref[0], rows, NT).astype(BF16)
        grad_ref[pl.ds(pl.multiple_of(h * tok + q * mt, mt), mt), :] = g

    @pl.loop(0, 4)
    def _(t):
        rows = group * slot
        place = place_ref[pl.ds(pl.multiple_of(t * rows, rows), rows), :]
        back = dot(place, grad_ref[...]).astype(BF16)
        back_ref[pl.ds(t * group, group)] = back.reshape(group, slot, half)

    ret_ref[s] = back_ref[s]

    @pl.loop(1, spans)
    def _(i):
        tok_copy(i).wait_recv()

    arrived = recv_ref[...].reshape(spans * slot, half)
    for t in range(4):
        block = dot(place_ref[:, t * 2 * mt : (t + 1) * 2 * mt], arrived, TN).astype(BF16)
        h, q = t // 2, 2 * (t % 2)
        merged_ref[:, q * dm + h * half : q * dm + (h + 1) * half] = block[:mt]
        merged_ref[:, (q + 1) * dm + h * half : (q + 1) * dm + (h + 1) * half] = block[mt:]

    blocks_ref[s] = merged_ref[:, pl.ds(pl.multiple_of(s * width, width), width)]

    @pl.loop(1, spans)
    def _(i):
        blk_copy(i).start()

    @pl.loop(1, spans)
    def _(i):
        back_copy(i).start()

    @pl.loop(0, 4)
    def _(t):
        at = pl.ds(pl.multiple_of(t * 256, 256), 256)
        o = dot(merged_ref[...], w_ref[:, at]) + bias_ref[0:1, at].astype(F32)
        merged_out_ref[0, :, at] = o.astype(BF16)

    @pl.loop(1, side)
    def _(i):
        two_x(i).wait_recv()
        two_y(i).wait_recv()

    cots_a = cot_a[...].reshape(spans * mt, half)
    cots_b = cot_b[...].reshape(spans * mt, half)
    ones = jnp.ones((8, spans * mt), BF16)
    sum_a = dot(ones, cots_a)
    sum_b = dot(ones, cots_b)
    lanes = 128
    for i in range(half // lanes):
        view_bias[v, i : i + 1, :] = sum_a[0:1, i * lanes : (i + 1) * lanes]
        view_bias[v, half // lanes + i : half // lanes + i + 1, :] = sum_b[
            0:1, i * lanes : (i + 1) * lanes
        ]

    @pl.loop(1, views)
    def _(i):
        bias_copy(i).start()

    @pl.loop(1, spans)
    def _(i):
        blk_copy(i).wait_recv()

    def product(h, to):
        lhs = blocks_ref[:, :, pl.ds(pl.multiple_of(h * hw, hw), hw)].reshape(spans * mt, hw)
        to[:, :half] = dot(lhs, cot_a[...].reshape(spans * mt, half), TN)
        to[:, half:] = dot(lhs, cot_b[...].reshape(spans * mt, half), TN)

    product(1 - core, half_send)
    pair.start()
    product(core, half_own)
    pair.wait_recv()
    half_own[...] += half_recv[...]

    @pl.loop(0, nz)
    def _(j):
        tv, ts = target(j)
        here = jnp.logical_and(tv == v, ts == s)

        @pl.when(jnp.logical_not(here))
        def _():
            fin_copy(j).start()

        @pl.when(here)
        def _():
            final_ref[z] = half_own[pl.ds(pl.multiple_of(j * part, part), part), :]

    @pl.loop(1, spans)
    def _(i):
        back_copy(i).wait_recv()

    returned = ret_ref[...].reshape(spans * slot, half)
    for t in range(2):
        g = dot(pick_ref[:, t * tok : (t + 1) * tok], returned, TN)
        token_grad_ref[0, :, t * half : (t + 1) * half] = g.astype(BF16)

    @pl.loop(1, views)
    def _(i):
        bias_copy(i).wait_recv()

    bias_grad_ref[...] = jnp.sum(view_bias[...], axis=0) * scale

    @pl.loop(0, nz)
    def _(k):
        tv, ts = source(k)

        @pl.when(jnp.logical_or(tv != v, ts != s))
        def _():
            fin_arrival(k).wait_recv()

    weight_grad_ref[...] = jnp.sum(final_ref[...], axis=0) * scale

    @pl.loop(1, spans)
    def _(i):
        tok_copy(i).wait_send()
        blk_copy(i).wait_send()
        back_copy(i).wait_send()

    @pl.loop(1, side)
    def _(i):
        one_y(i).wait_send()
        one_x(i).wait_send()
        two_x(i).wait_send()
        two_y(i).wait_send()

    @pl.loop(1, views)
    def _(i):
        bias_copy(i).wait_send()

    pair.wait_send()

    @pl.loop(0, nz)
    def _(j):
        tv, ts = target(j)

        @pl.when(jnp.logical_or(tv != v, ts != s))
        def _():
            fin_copy(j).wait_send()


def body(views, spans, tokens, scan_order, w_merge, bias, cotangent):
    tok, dm = tokens.shape[1:]
    merge_in, do = w_merge.shape
    mt = tok // 4
    half = dm // 2
    slot = 3 * (tok // spans)
    width = merge_in // spans
    part = merge_in // (views * spans)
    side = 4
    scale = 1.0 / math.sqrt(views * spans * mt)
    vmem = pl.BlockSpec(memory_space=pltpu.VMEM)
    dma = pltpu.SemaphoreType.DMA
    merged_out, token_grad, weight_grad, bias_grad = pl.pallas_call(
        functools.partial(kernel, views, spans, 128, scale),
        out_shape=(
            jax.ShapeDtypeStruct((1, mt, do), BF16),
            jax.ShapeDtypeStruct((1, tok, dm), BF16),
            jax.ShapeDtypeStruct((part, do), F32),
            jax.ShapeDtypeStruct((do // 128, 128), F32),
        ),
        in_specs=[vmem, vmem, pl.BlockSpec(memory_space=pl.ANY), vmem, vmem],
        out_specs=(vmem, vmem, vmem, vmem),
        scratch_shapes=[
            pltpu.VMEM((merge_in, do), BF16),
            pltpu.VMEM((spans, slot, half), BF16),
            pltpu.VMEM((spans, slot, half), BF16),
            pltpu.VMEM((spans, slot, half), BF16),
            pltpu.VMEM((spans, slot, half), BF16),
            pltpu.VMEM((spans * slot, 2 * tok), BF16),
            pltpu.VMEM((spans * slot, 2 * tok), BF16),
            pltpu.VMEM((spans, tok), F32),
            pltpu.VMEM((spans, tok), F32),
            pltpu.VMEM((mt, merge_in), BF16),
            pltpu.VMEM((2 * tok, half), BF16),
            pltpu.VMEM((spans, mt, width), BF16),
            pltpu.VMEM((side, side, mt, half), BF16),
            pltpu.VMEM((side, side, mt, half), BF16),
            pltpu.VMEM((width // 2, do), F32),
            pltpu.VMEM((width // 2, do), F32),
            pltpu.VMEM((width // 2, do), F32),
            pltpu.VMEM((views // 2, part, do), F32),
            pltpu.VMEM((views, do // 128, 128), F32),
            dma,
            dma((spans,)),
            dma((spans,)),
            dma((spans,)),
            dma((spans,)),
            dma((spans,)),
            dma((spans,)),
            dma((2 * side,)),
            dma((2 * side,)),
            dma((2 * side,)),
            dma((2 * side,)),
            dma((views,)),
            dma((views,)),
            dma((1,)),
            dma((1,)),
            dma((views // 2,)),
            dma((views // 2,)),
        ],
        compiler_params=pltpu.CompilerParams(
            collective_id=0, has_side_effects=True, vmem_limit_bytes=48 * 2**20
        ),
    )(tokens, scan_order, w_merge, bias.reshape(1, do), cotangent)
    return merged_out, token_grad, weight_grad, bias_grad.reshape(do)


def solution(mesh):
    in_specs = (P("view", "span", None), P("view", None), P(), P(), P("view", "span", None))
    out_specs = (P("view", "span", None), P("view", "span", None), P(("view", "span"), None), P())
    return jax.shard_map(
        functools.partial(body, mesh.shape["view"], mesh.shape["span"]),
        mesh=mesh,
        in_specs=in_specs,
        out_specs=out_specs,
        check_vma=False,
    )
```

```python
import functools
import math

import jax
import jax.numpy as jnp
from jax import lax
from jax.experimental import pallas as pl
from jax.experimental.pallas import tpu as pltpu
from jax.sharding import PartitionSpec as P

MESH = pl.DeviceIdType.MESH
F32 = jnp.float32
BF16 = jnp.bfloat16
NN = (((1,), (0,)), ((), ()))
NT = (((1,), (1,)), ((), ()))
TN = (((0,), (0,)), ((), ()))


def dot(a, b, dims=NN):
    return lax.dot_general(a, b, dims, preferred_element_type=F32)


def one_hot(hit):
    return jnp.where(hit, 1.0, 0.0).astype(BF16)


def kernel(
    views,
    spans,
    cols,
    scale,
    tokens_ref,
    order_ref,
    w_hbm,
    bias_ref,
    cot_ref,
    merged_out_ref,
    token_grad_ref,
    weight_grad_ref,
    bias_grad_ref,
    w_ref,
    out_ref,
    recv_ref,
    back_ref,
    ret_ref,
    pick_ref,
    place_ref,
    rank_ref,
    code_ref,
    merged_ref,
    grad_ref,
    blocks_ref,
    cot_all,
    prod_a,
    prod_b,
    in_a,
    in_b,
    part_a,
    part_b,
    last_a,
    last_b,
    span_bias,
    w_sem,
    tok_send,
    tok_recv,
    back_send,
    back_recv,
    blk_send,
    blk_recv,
    ring_send,
    ring_recv,
    share_send,
    share_recv,
    bias_send,
    bias_recv,
    sum_send,
    sum_recv,
    last_send,
    last_recv,
):
    v = lax.axis_index("view")
    s = lax.axis_index("span")
    core = lax.rem(v, 2)
    z = v // 2
    nz = views // 2
    steps = nz // 2
    side = 4
    x, y = s // side, lax.rem(s, side)
    tok = tokens_ref.shape[1]
    dm = tokens_ref.shape[2]
    half = dm // 2
    quarter = dm // 4
    mt = tok // 4
    cap = 3 * (tok // spans) // 2
    slot = 2 * cap
    width = blocks_ref.shape[2]
    groups = dm // width

    barrier = pltpu.get_barrier_semaphore()

    @pl.loop(1, spans)
    def _(i):
        pl.semaphore_signal(barrier, inc=1, device_id=(v, s ^ i), device_id_type=MESH)

    @pl.loop(1, views)
    def _(i):
        pl.semaphore_signal(barrier, inc=1, device_id=(v ^ i, s), device_id_type=MESH)

    w_copy = pltpu.make_async_copy(w_hbm, w_ref, w_sem)
    w_copy.start()

    def remote(src, dst, send, recv, device):
        return pltpu.make_async_remote_copy(
            src_ref=src,
            dst_ref=dst,
            send_sem=send,
            recv_sem=recv,
            device_id=device,
            device_id_type=MESH,
        )

    def tok_copy(h, i):
        at = h * spans + i
        return remote(
            out_ref.at[h, s ^ i], recv_ref.at[h, s], tok_send.at[at], tok_recv.at[at], (v, s ^ i)
        )

    def back_copy(i):
        return remote(
            back_ref.at[s ^ i], ret_ref.at[s], back_send.at[i], back_recv.at[i], (v, s ^ i)
        )

    def blk_copy(d):
        i = d ^ v
        src = merged_ref.at[:, pl.ds(pl.multiple_of(d * width, width), width)]
        return remote(src, blocks_ref.at[v], blk_send.at[i], blk_recv.at[i], (d, s))

    def near(k):
        return lax.rem(z + 2 * nz - k, nz)

    def ring_copy(way, k):
        held = near(k - 1) if way == 0 else near(1 - k)
        to = near(-1) if way == 0 else near(1)
        ref = cot_all.at[held, core]
        if k == steps:
            ref = ref.at[:, way * half : (way + 1) * half]
        at = way * (steps + 1) + k
        return remote(ref, ref, ring_send.at[at], ring_recv.at[at], (to * 2 + core, s))

    def share_copy(k):
        ref = cot_all.at[near(k), core]
        return remote(ref, ref, share_send.at[k], share_recv.at[k], (v ^ 1, s))

    def bias_copy(i):
        ref = span_bias.at[s]
        return remote(ref, ref, bias_send.at[i], bias_recv.at[i], (v, s ^ i))

    def sum_y(i):
        return remote(prod_a.at[:, y ^ i], in_a.at[y], sum_send.at[i], sum_recv.at[i], (v, s ^ i))

    def sum_x(i):
        at = side + i
        return remote(
            prod_b.at[x ^ i], in_b.at[x], sum_send.at[at], sum_recv.at[at], (v, s ^ (i * side))
        )

    def last_x(i):
        return remote(
            part_a.at[x ^ i], last_a.at[x], last_send.at[i], last_recv.at[i], (v, s ^ (i * side))
        )

    def last_y(i):
        at = side + i
        return remote(
            part_b.at[y ^ i], last_b.at[y], last_send.at[at], last_recv.at[at], (v, s ^ i)
        )

    before = one_hot(
        lax.broadcasted_iota(jnp.int32, (tok, tok), 0)
        < lax.broadcasted_iota(jnp.int32, (tok, tok), 1)
    )
    bits = int(math.log2(tok))
    mine = order_ref[0:1, pl.ds(pl.multiple_of(s * tok, tok), tok)]
    owner = lax.shift_right_logical(mine, bits)
    hot = jnp.where(lax.broadcasted_iota(jnp.int32, (spans, tok), 0) == owner, 1.0, 0.0)
    rank = jnp.sum(dot(hot.astype(BF16), before) * hot, axis=0, keepdims=True).astype(jnp.int32)
    first = owner * slot + rank
    slots = jnp.concatenate([first, first + cap], axis=1)

    cot_all[z, core] = cot_ref[0]
    group = spans // 4
    rows = group * slot

    def fill(h):
        @pl.loop(0, 4)
        def _(t):
            at = pl.ds(pl.multiple_of(t * rows, rows), rows)
            if h == 0:
                pick_ref[at, :] = one_hot(
                    lax.broadcasted_iota(jnp.int32, (rows, 2 * tok), 0) + t * rows == slots
                )
            c = h * half
            sent = dot(pick_ref[at, :tok], tokens_ref[0, :, c : c + quarter]) + dot(
                pick_ref[at, tok:], tokens_ref[0, :, c + quarter : c + half]
            )
            out_ref[h, pl.ds(t * group, group)] = sent.astype(BF16).reshape(group, slot, quarter)

        recv_ref[h, s] = out_ref[h, s]

    fill(0)
    pl.semaphore_wait(barrier, spans + views - 2)
    ring_copy(0, 1).start()
    ring_copy(1, 1).start()

    @pl.loop(1, spans)
    def _(i):
        tok_copy(0, i).start()

    share_copy(0).start()
    fill(1)

    @pl.loop(1, spans)
    def _(i):
        tok_copy(1, i).start()

    order = jnp.concatenate([order_ref[0:1, c * tok : (c + 1) * tok] for c in range(spans)], axis=0)
    arriving = lax.shift_right_logical(order, bits) == s
    arrive = jnp.where(arriving, 1.0, 0.0)
    rank_in = dot(arrive.astype(BF16), before)
    rank_ref[...] = jnp.where(arriving, rank_in, -1.0)
    local = lax.rem(order, tok)
    col = lax.rem(local, cols)
    quadrant = (local // cols) * 2 + lax.rem(col, 2)
    code_ref[...] = jnp.where(arriving, quadrant * mt + col // 2 + 1, 0).astype(F32)

    @pl.loop(0, spans)
    def _(c):
        rk = rank_ref[pl.ds(c, 1), :]
        cd = code_ref[pl.ds(c, 1), :]
        row = lax.broadcasted_iota(jnp.int32, (slot, tok), 0)
        k = jnp.where(row >= cap, row - cap, row).astype(F32)
        to = jnp.sum(jnp.where(rk == k, cd, 0.0), axis=1, keepdims=True).astype(jnp.int32)
        row = lax.broadcasted_iota(jnp.int32, (slot, 2 * tok), 0)
        lane = lax.broadcasted_iota(jnp.int32, (slot, 2 * tok), 1)
        wanted = jnp.where(row >= cap, lane - tok, lane) + 1
        wanted = jnp.where(wanted > tok, 0, wanted)
        place_ref[pl.ds(pl.multiple_of(c * slot, slot), slot), :] = one_hot(
            jnp.logical_and(to == wanted, wanted > 0)
        )

    def ring_step(k):
        ring_copy(0, k).wait_recv()
        ring_copy(1, k).wait_recv()
        if k < steps:
            ring_copy(0, k + 1).start()
            ring_copy(1, k + 1).start()
        share_copy(k).start()
        if k < steps:
            share_copy(nz - k).start()

    ring_step(1)
    w_copy.wait()

    @pl.loop(0, 8)
    def _(t):
        q, h = t // 2, lax.rem(t, 2)
        w_rows = w_ref[pl.ds(pl.multiple_of(t * half, half), half), :]
        g = dot(cot_ref[0], w_rows, NT).astype(BF16)
        grad_ref[pl.ds(pl.multiple_of(h * tok + q * mt, mt), mt), :] = g

    ring_step(2)

    @pl.loop(0, 4)
    def _(t):
        place = place_ref[pl.ds(pl.multiple_of(t * rows, rows), rows), :]
        back = dot(place, grad_ref[...]).astype(BF16)
        back_ref[pl.ds(t * group, group)] = back.reshape(group, slot, half)

    ret_ref[s] = back_ref[s]
    ring_step(3)

    def settle(h):
        @pl.loop(1, spans)
        def _(i):
            tok_copy(h, i).wait_recv()

        arrived = recv_ref[h].reshape(spans * slot, quarter)
        for t in range(4):
            block = dot(place_ref[:, t * 2 * mt : (t + 1) * 2 * mt], arrived, TN).astype(BF16)
            part, q = t // 2, 2 * (t % 2)
            c = q * dm + h * half + part * quarter
            merged_ref[:, c : c + quarter] = block[:mt]
            merged_ref[:, c + dm : c + dm + quarter] = block[mt:]

        @pl.loop(0, views // 2)
        def _(t):
            per = groups // 2
            d = (t // per) * groups + h * per + lax.rem(t, per)

            @pl.when(d != v)
            def _():
                blk_copy(d).start()

    settle(0)
    settle(1)
    blocks_ref[v] = merged_ref[:, pl.ds(pl.multiple_of(v * width, width), width)]

    @pl.loop(1, spans)
    def _(i):
        back_copy(i).start()

    @pl.loop(0, 4)
    def _(t):
        at = pl.ds(pl.multiple_of(t * 256, 256), 256)
        o = dot(merged_ref[...], w_ref[:, at]) + bias_ref[0:1, at].astype(F32)
        merged_out_ref[0, :, at] = o.astype(BF16)

    ring_step(4)

    @pl.loop(0, nz)
    def _(k):
        share_copy(k).wait_recv()

    depth = views * mt
    lanes = 128
    sums = dot(jnp.ones((8, depth), BF16), cot_all[...].reshape(depth, dm))
    for i in range(dm // lanes):
        span_bias[s, i : i + 1, :] = sums[0:1, i * lanes : (i + 1) * lanes]

    @pl.loop(1, spans)
    def _(i):
        bias_copy(i).start()

    @pl.loop(1, views)
    def _(i):
        blk_copy(v ^ i).wait_recv()

    lhs = blocks_ref[...].reshape(depth, width)
    prod_a[...] = dot(lhs, cot_all[:, :, :, :half].reshape(depth, half), TN).reshape(prod_a.shape)

    @pl.loop(1, side)
    def _(i):
        sum_y(i).start()

    prod_b[...] = dot(lhs, cot_all[:, :, :, half:].reshape(depth, half), TN).reshape(prod_b.shape)

    @pl.loop(1, side)
    def _(i):
        sum_x(i).start()

    in_a[y] = prod_a[:, y]
    in_b[x] = prod_b[x]

    @pl.loop(1, side)
    def _(i):
        sum_y(i).wait_recv()

    part_a[...] = jnp.sum(in_a[...], axis=0)
    last_a[x] = part_a[x]

    @pl.loop(1, side)
    def _(i):
        last_x(i).start()

    @pl.loop(1, side)
    def _(i):
        sum_x(i).wait_recv()

    part_b[...] = jnp.sum(in_b[...], axis=0)
    last_b[y] = part_b[y]

    @pl.loop(1, side)
    def _(i):
        last_y(i).start()

    @pl.loop(1, spans)
    def _(i):
        back_copy(i).wait_recv()

    returned = ret_ref[...].reshape(spans * slot, half)
    for t in range(2):
        g = dot(pick_ref[:, t * tok : (t + 1) * tok], returned, TN)
        token_grad_ref[0, :, t * half : (t + 1) * half] = g.astype(BF16)

    @pl.loop(1, spans)
    def _(i):
        bias_copy(i).wait_recv()

    bias_grad_ref[...] = jnp.sum(span_bias[...], axis=0) * scale

    @pl.loop(1, side)
    def _(i):
        last_x(i).wait_recv()
        last_y(i).wait_recv()

    weight_grad_ref[:, :half] = jnp.sum(last_a[...], axis=0) * scale
    weight_grad_ref[:, half:] = jnp.sum(last_b[...], axis=0) * scale

    @pl.loop(1, spans)
    def _(i):
        tok_copy(0, i).wait_send()
        tok_copy(1, i).wait_send()
        back_copy(i).wait_send()
        bias_copy(i).wait_send()

    @pl.loop(1, views)
    def _(i):
        blk_copy(v ^ i).wait_send()

    for k in range(1, steps + 1):
        ring_copy(0, k).wait_send()
        ring_copy(1, k).wait_send()

    @pl.loop(0, nz)
    def _(k):
        share_copy(k).wait_send()

    @pl.loop(1, side)
    def _(i):
        sum_y(i).wait_send()
        sum_x(i).wait_send()
        last_x(i).wait_send()
        last_y(i).wait_send()


def body(views, spans, tokens, scan_order, w_merge, bias, cotangent):
    tok, dm = tokens.shape[1:]
    merge_in, do = w_merge.shape
    mt = tok // 4
    half, quarter = dm // 2, dm // 4
    slot = 3 * (tok // spans)
    width = merge_in // views
    part = merge_in // (views * spans)
    side = 4
    nz = views // 2
    scale = 1.0 / math.sqrt(views * spans * mt)
    vmem = pl.BlockSpec(memory_space=pltpu.VMEM)
    dma = pltpu.SemaphoreType.DMA
    merged_out, token_grad, weight_grad, bias_grad = pl.pallas_call(
        functools.partial(kernel, views, spans, 128, scale),
        out_shape=(
            jax.ShapeDtypeStruct((1, mt, do), BF16),
            jax.ShapeDtypeStruct((1, tok, dm), BF16),
            jax.ShapeDtypeStruct((part, do), F32),
            jax.ShapeDtypeStruct((do // 128, 128), F32),
        ),
        in_specs=[vmem, vmem, pl.BlockSpec(memory_space=pl.ANY), vmem, vmem],
        out_specs=(vmem, vmem, vmem, vmem),
        scratch_shapes=[
            pltpu.VMEM((merge_in, do), BF16),
            pltpu.VMEM((2, spans, slot, quarter), BF16),
            pltpu.VMEM((2, spans, slot, quarter), BF16),
            pltpu.VMEM((spans, slot, half), BF16),
            pltpu.VMEM((spans, slot, half), BF16),
            pltpu.VMEM((spans * slot, 2 * tok), BF16),
            pltpu.VMEM((spans * slot, 2 * tok), BF16),
            pltpu.VMEM((spans, tok), F32),
            pltpu.VMEM((spans, tok), F32),
            pltpu.VMEM((mt, merge_in), BF16),
            pltpu.VMEM((2 * tok, half), BF16),
            pltpu.VMEM((views, mt, width), BF16),
            pltpu.VMEM((nz, 2, mt, do), BF16),
            pltpu.VMEM((side, side, part, half), F32),
            pltpu.VMEM((side, side, part, half), F32),
            pltpu.VMEM((side, side, part, half), F32),
            pltpu.VMEM((side, side, part, half), F32),
            pltpu.VMEM((side, part, half), F32),
            pltpu.VMEM((side, part, half), F32),
            pltpu.VMEM((side, part, half), F32),
            pltpu.VMEM((side, part, half), F32),
            pltpu.VMEM((spans, do // 128, 128), F32),
            dma,
            dma((2 * spans,)),
            dma((2 * spans,)),
            dma((spans,)),
            dma((spans,)),
            dma((views,)),
            dma((views,)),
            dma((nz + 2,)),
            dma((nz + 2,)),
            dma((nz,)),
            dma((nz,)),
            dma((spans,)),
            dma((spans,)),
            dma((2 * side,)),
            dma((2 * side,)),
            dma((2 * side,)),
            dma((2 * side,)),
        ],
        compiler_params=pltpu.CompilerParams(
            collective_id=0, has_side_effects=True, vmem_limit_bytes=48 * 2**20
        ),
    )(tokens, scan_order, w_merge, bias.reshape(1, do), cotangent)
    return merged_out, token_grad, weight_grad, bias_grad.reshape(do)


def solution(mesh):
    in_specs = (P("view", "span", None), P("view", None), P(), P(), P("view", "span", None))
    out_specs = (P("view", "span", None), P("view", "span", None), P(("view", "span"), None), P())
    return jax.shard_map(
        functools.partial(body, mesh.shape["view"], mesh.shape["span"]),
        mesh=mesh,
        in_specs=in_specs,
        out_specs=out_specs,
        check_vma=False,
    )
```

```python
import functools
import math

import jax
import jax.numpy as jnp
from jax import lax
from jax.experimental import pallas as pl
from jax.experimental.pallas import tpu as pltpu
from jax.sharding import PartitionSpec as P

MESH = pl.DeviceIdType.MESH
F32 = jnp.float32
BF16 = jnp.bfloat16
NN = (((1,), (0,)), ((), ()))
NT = (((1,), (1,)), ((), ()))
TN = (((0,), (0,)), ((), ()))


def dot(a, b, dims=NN):
    return lax.dot_general(a, b, dims, preferred_element_type=F32)


def one_hot(hit):
    return jnp.where(hit, 1.0, 0.0).astype(BF16)


def kernel(
    views,
    spans,
    cols,
    scale,
    tokens_hbm,
    order_hbm,
    w_hbm,
    bias_ref,
    cot_hbm,
    merged_out_ref,
    token_grad_ref,
    weight_grad_ref,
    bias_grad_ref,
    w_ref,
    tokens_ref,
    order_ref,
    out_ref,
    recv_ref,
    back_ref,
    ret_ref,
    pick_ref,
    place_ref,
    rank_ref,
    code_ref,
    merged_ref,
    grad_ref,
    blocks_ref,
    cot_all,
    prod_a,
    prod_b,
    in_a,
    in_b,
    part_a,
    part_b,
    last_a,
    last_b,
    span_bias,
    in_sem,
    tok_send,
    tok_recv,
    back_send,
    back_recv,
    blk_send,
    blk_recv,
    ring_send,
    ring_recv,
    share_send,
    share_recv,
    bias_send,
    bias_recv,
    sum_a_send,
    sum_a_recv,
    sum_b_send,
    sum_b_recv,
    last_a_send,
    last_a_recv,
    last_b_send,
    last_b_recv,
):
    v = lax.axis_index("view")
    s = lax.axis_index("span")
    core = lax.rem(v, 2)
    z = v // 2
    nz = views // 2
    steps = nz // 2
    side = 4
    x, y = s // side, lax.rem(s, side)
    mine_half = x // 2
    tok, dm = tokens_ref.shape
    half = dm // 2
    mt = tok // 4
    cap = 3 * (tok // spans) // 2
    slot = 2 * cap
    lanes = blocks_ref.shape[3]
    width = 2 * lanes
    na = prod_a.shape[4]

    order_in = pltpu.make_async_copy(order_hbm, order_ref, in_sem.at[0])
    tokens_in = pltpu.make_async_copy(tokens_hbm.at[0], tokens_ref, in_sem.at[1])
    cot_in = pltpu.make_async_copy(cot_hbm.at[0], cot_all.at[z, core], in_sem.at[2])
    w_in = pltpu.make_async_copy(w_hbm, w_ref, in_sem.at[3])
    order_in.start()
    tokens_in.start()
    cot_in.start()

    barrier = pltpu.get_barrier_semaphore()

    @pl.loop(1, spans)
    def _(i):
        pl.semaphore_signal(barrier, inc=1, device_id=(v, s ^ i), device_id_type=MESH)

    @pl.loop(1, views)
    def _(i):
        pl.semaphore_signal(barrier, inc=1, device_id=(v ^ i, s), device_id_type=MESH)

    w_in.start()

    def remote(src, dst, send, recv, device):
        return pltpu.make_async_remote_copy(
            src_ref=src,
            dst_ref=dst,
            send_sem=send,
            recv_sem=recv,
            device_id=device,
            device_id_type=MESH,
        )

    def tok_copy(h, i):
        at = h * spans + i
        return remote(
            out_ref.at[h, s ^ i], recv_ref.at[h, s], tok_send.at[at], tok_recv.at[at], (v, s ^ i)
        )

    def back_copy(i):
        return remote(
            back_ref.at[s ^ i], ret_ref.at[s], back_send.at[i], back_recv.at[i], (v, s ^ i)
        )

    def blk_copy(h, i):
        d = v ^ i
        at = h * views + i
        src = merged_ref.at[:, pl.ds(pl.multiple_of(d * width + h * lanes, lanes), lanes)]
        return remote(src, blocks_ref.at[h, v], blk_send.at[at], blk_recv.at[at], (d, s))

    def near(k):
        return lax.rem(z + 2 * nz - k, nz)

    def ring_copy(way, k):
        held = near(k - 1) if way == 0 else near(1 - k)
        to = near(-1) if way == 0 else near(1)
        ref = cot_all.at[held, core]
        if k == steps:
            ref = ref.at[:, way * half : (way + 1) * half]
        at = way * (steps + 1) + k
        return remote(ref, ref, ring_send.at[at], ring_recv.at[at], (to * 2 + core, s))

    def share_copy(k):
        ref = cot_all.at[near(k), core]
        return remote(ref, ref, share_send.at[k], share_recv.at[k], (v ^ 1, s))

    def bias_copy(i):
        ref = span_bias.at[s]
        return remote(ref, ref, bias_send.at[i], bias_recv.at[i], (v, s ^ i))

    def sum_a(h, i):
        at = h * side + i
        return remote(
            prod_a.at[h, :, y ^ i], in_a.at[h, y], sum_a_send.at[at], sum_a_recv.at[at], (v, s ^ i)
        )

    def sum_b(h, t, k):
        to = (2 * h + t) * side + y
        return remote(
            prod_b.at[h, t], in_b.at[k], sum_b_send.at[2 * h + t], sum_b_recv.at[k], (v, to)
        )

    def last_a_copy(h, t, k):
        to = (2 * h + t) * side + y
        return remote(
            part_a.at[h, t], last_a.at[k], last_a_send.at[2 * h + t], last_a_recv.at[k], (v, to)
        )

    def last_b_copy(i):
        return remote(
            part_b.at[y ^ i], last_b.at[y], last_b_send.at[i], last_b_recv.at[i], (v, s ^ i)
        )

    def pair_up(rows):
        n = rows.shape[1] // 2
        a = rows[:, :n].reshape(spans, cap, n)
        b = rows[:, n:].reshape(spans, cap, n)
        return jnp.concatenate([a, b], axis=1).astype(BF16)

    def unpair(slots):
        wide = slots.astype(F32)
        n = wide.shape[2]
        a = wide[:, :cap].reshape(spans * cap, n)
        b = wide[:, cap:].reshape(spans * cap, n)
        return jnp.concatenate([a, b], axis=1).astype(BF16)

    before = one_hot(
        lax.broadcasted_iota(jnp.int32, (tok, tok), 0)
        < lax.broadcasted_iota(jnp.int32, (tok, tok), 1)
    )
    bits = int(math.log2(tok))
    order_in.wait()
    mine = order_ref[0:1, pl.ds(pl.multiple_of(s * tok, tok), tok)]
    owner = lax.shift_right_logical(mine, bits)
    hot = jnp.where(lax.broadcasted_iota(jnp.int32, (spans, tok), 0) == owner, 1.0, 0.0)
    rank = jnp.sum(dot(hot.astype(BF16), before) * hot, axis=0, keepdims=True).astype(jnp.int32)
    to_slot = owner * cap + rank
    pick_ref[...] = one_hot(lax.broadcasted_iota(jnp.int32, (spans * cap, tok), 0) == to_slot)
    tokens_in.wait()

    def pieces(h):
        return [c + h * lanes for c in range(0, dm, width)]

    def fill(h):
        part = jnp.concatenate([tokens_ref[:, c : c + lanes] for c in pieces(h)], axis=1)
        out_ref[h] = pair_up(dot(pick_ref[...], part))
        recv_ref[h, s] = out_ref[h, s]

    fill(0)
    cot_in.wait()
    pl.semaphore_wait(barrier, spans + views - 2)
    ring_copy(0, 1).start()
    ring_copy(1, 1).start()

    @pl.loop(1, spans)
    def _(i):
        tok_copy(0, i).start()

    share_copy(0).start()
    fill(1)

    @pl.loop(1, spans)
    def _(i):
        tok_copy(1, i).start()

    order = jnp.concatenate([order_ref[0:1, c * tok : (c + 1) * tok] for c in range(spans)], axis=0)
    arriving = lax.shift_right_logical(order, bits) == s
    arrive = jnp.where(arriving, 1.0, 0.0)
    rank_in = dot(arrive.astype(BF16), before)
    rank_ref[...] = jnp.where(arriving, rank_in, -1.0)
    local = lax.rem(order, tok)
    col = lax.rem(local, cols)
    quadrant = (local // cols) * 2 + lax.rem(col, 2)
    code_ref[...] = jnp.where(arriving, quadrant * mt + col // 2 + 1, 0).astype(F32)

    @pl.loop(0, spans // 2)
    def _(t):
        k = lax.broadcasted_iota(jnp.int32, (cap, tok), 0).astype(F32)
        lane = lax.broadcasted_iota(jnp.int32, (cap, tok), 1).astype(F32) + 1.0
        found = []
        for c in range(2):
            rk = rank_ref[pl.ds(2 * t + c, 1), :]
            cd = code_ref[pl.ds(2 * t + c, 1), :]
            to = jnp.sum(jnp.where(rk == k, cd, 0.0), axis=1, keepdims=True)
            found.append(jnp.where(to == lane, 1.0, 0.0))
        place_ref[pl.ds(pl.multiple_of(t * slot, slot), slot), :] = jnp.concatenate(
            found, axis=0
        ).astype(BF16)

    def ring_step(k):
        ring_copy(0, k).wait_recv()
        ring_copy(1, k).wait_recv()
        if k < steps:
            ring_copy(0, k + 1).start()
            ring_copy(1, k + 1).start()
        share_copy(k).start()
        if k < steps:
            share_copy(nz - k).start()

    ring_step(1)
    w_in.wait()

    @pl.loop(0, 4)
    def _(q):
        w_rows = w_ref[pl.ds(pl.multiple_of(q * dm, dm), dm), :]
        g = dot(cot_all[z, core], w_rows, NT).astype(BF16)
        grad_ref[pl.ds(pl.multiple_of(q * mt, mt), mt), :] = g

    ring_step(2)

    def settle(h):
        @pl.loop(1, spans)
        def _(i):
            tok_copy(h, i).wait_recv()

        block = dot(place_ref[...], unpair(recv_ref[h]), TN).astype(BF16)
        for q in range(4):
            for n, c in enumerate(pieces(h)):
                merged_ref[:, q * dm + c : q * dm + c + lanes] = block[
                    q * mt : (q + 1) * mt, n * lanes : (n + 1) * lanes
                ]
        at = pl.ds(pl.multiple_of(v * width + h * lanes, lanes), lanes)
        blocks_ref[h, v] = merged_ref[:, at]

        @pl.loop(1, views)
        def _(i):
            blk_copy(h, i).start()

    settle(0)
    ring_step(3)
    back_ref[...] = pair_up(dot(place_ref[...], grad_ref[...]))
    ret_ref[s] = back_ref[s]
    settle(1)

    @pl.loop(1, spans)
    def _(i):
        back_copy(i).start()

    @pl.loop(0, 4)
    def _(t):
        at = pl.ds(pl.multiple_of(t * 256, 256), 256)
        o = dot(merged_ref[...], w_ref[:, at]) + bias_ref[0:1, at].astype(F32)
        merged_out_ref[0, :, at] = o.astype(BF16)

    ring_step(4)

    @pl.loop(0, nz)
    def _(k):
        share_copy(k).wait_recv()

    depth = views * mt

    def multiply(h):
        @pl.loop(1, views)
        def _(i):
            blk_copy(h, i).wait_recv()

        lhs = blocks_ref[h].reshape(depth, lanes)
        prod_a[h] = dot(lhs, cot_all[:, :, :, :na].reshape(depth, na), TN).reshape(
            prod_a.shape[1:]
        )

        @pl.loop(1, side)
        def _(i):
            sum_a(h, i).start()

        prod_b[h] = dot(lhs, cot_all[:, :, :, na:].reshape(depth, dm - na), TN).reshape(
            prod_b.shape[1:]
        )
        for t in range(2):

            @pl.when(x != 2 * h + t)
            def _():
                sum_b(h, t, x).start()

            @pl.when(x == 2 * h + t)
            def _():
                in_b[x] = prod_b[h, t]

        in_a[h, y] = prod_a[h, :, y]

    def combine(h):
        @pl.loop(1, side)
        def _(i):
            sum_a(h, i).wait_recv()

        part_a[h] = jnp.sum(in_a[h], axis=0)
        for t in range(2):

            @pl.when(x != 2 * h + t)
            def _():
                last_a_copy(h, t, x).start()

            @pl.when(x == 2 * h + t)
            def _():
                last_a[x] = part_a[h, t]

        @pl.when(mine_half == h)
        def _():
            @pl.loop(1, side)
            def _(i):
                sum_b(h, 0, x ^ i).wait_recv()

            part_b[...] = jnp.sum(in_b[...], axis=0)
            last_b[y] = part_b[y]

            @pl.loop(1, side)
            def _(i):
                last_b_copy(i).start()

    multiply(0)

    sums = dot(jnp.ones((8, depth), BF16), cot_all[...].reshape(depth, dm))
    for i in range(dm // 128):
        span_bias[s, i : i + 1, :] = sums[0:1, i * 128 : (i + 1) * 128]

    @pl.loop(1, spans)
    def _(i):
        bias_copy(i).start()

    multiply(1)
    combine(0)
    combine(1)

    @pl.loop(1, spans)
    def _(i):
        back_copy(i).wait_recv()

    token_grad_ref[0] = dot(pick_ref[...], unpair(ret_ref[...]), TN).astype(BF16)

    @pl.loop(1, spans)
    def _(i):
        bias_copy(i).wait_recv()

    bias_grad_ref[...] = jnp.sum(span_bias[...], axis=0) * scale

    @pl.loop(1, side)
    def _(i):
        last_a_copy(0, 0, x ^ i).wait_recv()
        last_b_copy(i).wait_recv()

    weight_grad_ref[:, :na] = jnp.sum(last_a[...], axis=0) * scale
    weight_grad_ref[:, na:] = jnp.sum(last_b[...], axis=0) * scale

    @pl.loop(1, spans)
    def _(i):
        tok_copy(0, i).wait_send()
        tok_copy(1, i).wait_send()
        back_copy(i).wait_send()
        bias_copy(i).wait_send()

    @pl.loop(1, views)
    def _(i):
        blk_copy(0, i).wait_send()
        blk_copy(1, i).wait_send()

    for k in range(1, steps + 1):
        ring_copy(0, k).wait_send()
        ring_copy(1, k).wait_send()

    @pl.loop(0, nz)
    def _(k):
        share_copy(k).wait_send()

    @pl.loop(1, side)
    def _(i):
        sum_a(0, i).wait_send()
        sum_a(1, i).wait_send()
        last_b_copy(i).wait_send()

    for h in range(2):
        for t in range(2):

            @pl.when(x != 2 * h + t)
            def _():
                sum_b(h, t, x).wait_send()
                last_a_copy(h, t, x).wait_send()


def body(views, spans, tokens, scan_order, w_merge, bias, cotangent):
    tok, dm = tokens.shape[1:]
    merge_in, do = w_merge.shape
    mt = tok // 4
    half = dm // 2
    cap = 3 * (tok // spans) // 2
    slot = 2 * cap
    lanes = merge_in // views // 2
    part = merge_in // (views * spans)
    side = 4
    nz = views // 2
    na = 5 * do // 8
    nb = do - na
    scale = 1.0 / math.sqrt(views * spans * mt)
    vmem = pl.BlockSpec(memory_space=pltpu.VMEM)
    hbm = pl.BlockSpec(memory_space=pl.ANY)
    dma = pltpu.SemaphoreType.DMA
    merged_out, token_grad, weight_grad, bias_grad = pl.pallas_call(
        functools.partial(kernel, views, spans, 128, scale),
        out_shape=(
            jax.ShapeDtypeStruct((1, mt, do), BF16),
            jax.ShapeDtypeStruct((1, tok, dm), BF16),
            jax.ShapeDtypeStruct((part, do), F32),
            jax.ShapeDtypeStruct((do // 128, 128), F32),
        ),
        in_specs=[hbm, hbm, hbm, vmem, hbm],
        out_specs=(vmem, vmem, vmem, vmem),
        scratch_shapes=[
            pltpu.VMEM((merge_in, do), BF16),
            pltpu.VMEM((tok, dm), BF16),
            pltpu.VMEM((1, spans * tok), jnp.int32),
            pltpu.VMEM((2, spans, slot, half // 2), BF16),
            pltpu.VMEM((2, spans, slot, half // 2), BF16),
            pltpu.VMEM((spans, slot, half), BF16),
            pltpu.VMEM((spans, slot, half), BF16),
            pltpu.VMEM((spans * cap, tok), BF16),
            pltpu.VMEM((spans * cap, tok), BF16),
            pltpu.VMEM((spans, tok), F32),
            pltpu.VMEM((spans, tok), F32),
            pltpu.VMEM((mt, merge_in), BF16),
            pltpu.VMEM((tok, dm), BF16),
            pltpu.VMEM((2, views, mt, lanes), BF16),
            pltpu.VMEM((nz, 2, mt, do), BF16),
            pltpu.VMEM((2, 2, side, part, na), F32),
            pltpu.VMEM((2, 2, side, part, nb), F32),
            pltpu.VMEM((2, side, 2, part, na), F32),
            pltpu.VMEM((side, side, part, nb), F32),
            pltpu.VMEM((2, 2, part, na), F32),
            pltpu.VMEM((side, part, nb), F32),
            pltpu.VMEM((side, part, na), F32),
            pltpu.VMEM((side, part, nb), F32),
            pltpu.VMEM((spans, do // 128, 128), F32),
            dma((4,)),
            dma((2 * spans,)),
            dma((2 * spans,)),
            dma((spans,)),
            dma((spans,)),
            dma((2 * views,)),
            dma((2 * views,)),
            dma((nz + 2,)),
            dma((nz + 2,)),
            dma((nz,)),
            dma((nz,)),
            dma((spans,)),
            dma((spans,)),
            dma((2 * side,)),
            dma((2 * side,)),
            dma((side,)),
            dma((side,)),
            dma((side,)),
            dma((side,)),
            dma((side,)),
            dma((side,)),
        ],
        compiler_params=pltpu.CompilerParams(
            collective_id=0, has_side_effects=True, vmem_limit_bytes=60 * 2**20
        ),
    )(tokens, scan_order, w_merge, bias.reshape(1, do), cotangent)
    return merged_out, token_grad, weight_grad, bias_grad.reshape(do)


def solution(mesh):
    in_specs = (P("view", "span", None), P("view", None), P(), P(), P("view", "span", None))
    out_specs = (P("view", "span", None), P("view", "span", None), P(("view", "span"), None), P())
    return jax.shard_map(
        functools.partial(body, mesh.shape["view"], mesh.shape["span"]),
        mesh=mesh,
        in_specs=in_specs,
        out_specs=out_specs,
        check_vma=False,
    )
```

```python
import functools
import math

import jax
import jax.numpy as jnp
from jax import lax
from jax.experimental import pallas as pl
from jax.experimental.pallas import tpu as pltpu
from jax.sharding import PartitionSpec as P

MESH = pl.DeviceIdType.MESH
F32 = jnp.float32
BF16 = jnp.bfloat16
NN = (((1,), (0,)), ((), ()))
NT = (((1,), (1,)), ((), ()))
TN = (((0,), (0,)), ((), ()))


def dot(a, b, dims=NN):
    return lax.dot_general(a, b, dims, preferred_element_type=F32)


def one_hot(hit):
    return jnp.where(hit, 1.0, 0.0).astype(BF16)


def kernel(
    views,
    spans,
    cols,
    scale,
    tokens_hbm,
    order_hbm,
    w_hbm,
    bias_hbm,
    cot_hbm,
    merged_out_hbm,
    token_grad_hbm,
    weight_grad_hbm,
    bias_grad_hbm,
    merged_out_ref,
    token_grad_ref,
    weight_grad_ref,
    bias_grad_ref,
    w_ref,
    tokens_ref,
    order_ref,
    bias_ref,
    out_ref,
    recv_ref,
    back_ref,
    ret_ref,
    pick_ref,
    place_ref,
    rank_ref,
    code_ref,
    merged_ref,
    grad_ref,
    blocks_ref,
    cot_all,
    prod_a,
    prod_b,
    in_a,
    in_b,
    part_a,
    part_b,
    last_a,
    last_b,
    span_bias,
    in_sem,
    tok_send,
    tok_recv,
    back_send,
    back_recv,
    blk_send,
    blk_recv,
    ring_send,
    ring_recv,
    share_send,
    share_recv,
    bias_send,
    bias_recv,
    sum_a_send,
    sum_a_recv,
    sum_b_send,
    sum_b_recv,
    last_a_send,
    last_a_recv,
    last_b_send,
    last_b_recv,
):
    v = lax.axis_index("view")
    s = lax.axis_index("span")
    core = lax.rem(v, 2)
    z = v // 2
    nz = views // 2
    steps = nz // 2
    side = 4
    x, y = s // side, lax.rem(s, side)
    mine_half = x // 2
    tok, dm = tokens_ref.shape
    half = dm // 2
    mt = tok // 4
    cap = 3 * (tok // spans) // 2
    slot = 2 * cap
    lanes = blocks_ref.shape[3]
    width = 2 * lanes
    na = prod_a.shape[4]

    order_in = pltpu.make_async_copy(order_hbm, order_ref, in_sem.at[0])
    tokens_in = pltpu.make_async_copy(tokens_hbm.at[0], tokens_ref, in_sem.at[1])
    cot_in = pltpu.make_async_copy(cot_hbm.at[0], cot_all.at[z, core], in_sem.at[2])
    w_in = pltpu.make_async_copy(w_hbm, w_ref, in_sem.at[3])
    bias_in = pltpu.make_async_copy(bias_hbm, bias_ref, in_sem.at[4])
    merged_put = pltpu.make_async_copy(merged_out_ref, merged_out_hbm, in_sem.at[5])
    tokens_put = pltpu.make_async_copy(token_grad_ref, token_grad_hbm, in_sem.at[6])
    weight_put = pltpu.make_async_copy(weight_grad_ref, weight_grad_hbm, in_sem.at[7])
    bias_put = pltpu.make_async_copy(bias_grad_ref, bias_grad_hbm, in_sem.at[8])
    order_in.start()
    tokens_in.start()
    cot_in.start()

    barrier = pltpu.get_barrier_semaphore()

    @pl.loop(1, spans)
    def _(i):
        pl.semaphore_signal(barrier, inc=1, device_id=(v, s ^ i), device_id_type=MESH)

    @pl.loop(1, views)
    def _(i):
        pl.semaphore_signal(barrier, inc=1, device_id=(v ^ i, s), device_id_type=MESH)

    w_in.start()
    bias_in.start()

    def remote(src, dst, send, recv, device):
        return pltpu.make_async_remote_copy(
            src_ref=src,
            dst_ref=dst,
            send_sem=send,
            recv_sem=recv,
            device_id=device,
            device_id_type=MESH,
        )

    def tok_copy(h, i):
        at = h * spans + i
        return remote(
            out_ref.at[h, s ^ i], recv_ref.at[h, s], tok_send.at[at], tok_recv.at[at], (v, s ^ i)
        )

    def back_copy(i):
        return remote(
            back_ref.at[s ^ i], ret_ref.at[s], back_send.at[i], back_recv.at[i], (v, s ^ i)
        )

    def blk_copy(h, i):
        d = v ^ i
        at = h * views + i
        src = merged_ref.at[:, pl.ds(pl.multiple_of(d * width + h * lanes, lanes), lanes)]
        return remote(src, blocks_ref.at[h, v], blk_send.at[at], blk_recv.at[at], (d, s))

    def near(k):
        return lax.rem(z + 2 * nz - k, nz)

    def ring_copy(way, k):
        held = near(k - 1) if way == 0 else near(1 - k)
        to = near(-1) if way == 0 else near(1)
        ref = cot_all.at[held, core]
        if k == steps:
            ref = ref.at[:, way * half : (way + 1) * half]
        at = way * (steps + 1) + k
        return remote(ref, ref, ring_send.at[at], ring_recv.at[at], (to * 2 + core, s))

    def share_copy(k):
        ref = cot_all.at[near(k), core]
        return remote(ref, ref, share_send.at[k], share_recv.at[k], (v ^ 1, s))

    def bias_copy(i):
        ref = span_bias.at[s]
        return remote(ref, ref, bias_send.at[i], bias_recv.at[i], (v, s ^ i))

    def sum_a(h, i):
        at = h * side + i
        return remote(
            prod_a.at[h, :, y ^ i], in_a.at[h, y], sum_a_send.at[at], sum_a_recv.at[at], (v, s ^ i)
        )

    def sum_b(h, t, k):
        to = (2 * h + t) * side + y
        return remote(
            prod_b.at[h, t], in_b.at[k], sum_b_send.at[2 * h + t], sum_b_recv.at[k], (v, to)
        )

    def last_a_copy(h, t, k):
        to = (2 * h + t) * side + y
        return remote(
            part_a.at[h, t], last_a.at[k], last_a_send.at[2 * h + t], last_a_recv.at[k], (v, to)
        )

    def last_b_copy(i):
        return remote(
            part_b.at[y ^ i], last_b.at[y], last_b_send.at[i], last_b_recv.at[i], (v, s ^ i)
        )

    def pair_up(rows):
        n = rows.shape[1] // 2
        a = rows[:, :n].reshape(spans, cap, n)
        b = rows[:, n:].reshape(spans, cap, n)
        return jnp.concatenate([a, b], axis=1).astype(BF16)

    def unpair(slots):
        wide = slots.astype(F32)
        n = wide.shape[2]
        a = wide[:, :cap].reshape(spans * cap, n)
        b = wide[:, cap:].reshape(spans * cap, n)
        return jnp.concatenate([a, b], axis=1).astype(BF16)

    before = one_hot(
        lax.broadcasted_iota(jnp.int32, (tok, tok), 0)
        < lax.broadcasted_iota(jnp.int32, (tok, tok), 1)
    )
    bits = int(math.log2(tok))
    order_in.wait()
    mine = order_ref[0:1, pl.ds(pl.multiple_of(s * tok, tok), tok)]
    owner = lax.shift_right_logical(mine, bits)
    hot = jnp.where(lax.broadcasted_iota(jnp.int32, (spans, tok), 0) == owner, 1.0, 0.0)
    rank = jnp.sum(dot(hot.astype(BF16), before) * hot, axis=0, keepdims=True).astype(jnp.int32)
    to_slot = owner * cap + rank
    pick_ref[...] = one_hot(lax.broadcasted_iota(jnp.int32, (spans * cap, tok), 0) == to_slot)
    tokens_in.wait()

    def pieces(h):
        return [c + h * lanes for c in range(0, dm, width)]

    def fill(h):
        part = jnp.concatenate([tokens_ref[:, c : c + lanes] for c in pieces(h)], axis=1)
        out_ref[h] = pair_up(dot(pick_ref[...], part))
        recv_ref[h, s] = out_ref[h, s]

    fill(0)
    cot_in.wait()
    pl.semaphore_wait(barrier, spans + views - 2)
    ring_copy(0, 1).start()
    ring_copy(1, 1).start()

    @pl.loop(1, spans)
    def _(i):
        tok_copy(0, i).start()

    share_copy(0).start()
    fill(1)

    @pl.loop(1, spans)
    def _(i):
        tok_copy(1, i).start()

    order = jnp.concatenate([order_ref[0:1, c * tok : (c + 1) * tok] for c in range(spans)], axis=0)
    arriving = lax.shift_right_logical(order, bits) == s
    arrive = jnp.where(arriving, 1.0, 0.0)
    rank_in = dot(arrive.astype(BF16), before)
    rank_ref[...] = jnp.where(arriving, rank_in, -1.0)
    local = lax.rem(order, tok)
    col = lax.rem(local, cols)
    quadrant = (local // cols) * 2 + lax.rem(col, 2)
    code_ref[...] = jnp.where(arriving, quadrant * mt + col // 2 + 1, 0).astype(F32)

    @pl.loop(0, spans // 2)
    def _(t):
        k = lax.broadcasted_iota(jnp.int32, (cap, tok), 0).astype(F32)
        lane = lax.broadcasted_iota(jnp.int32, (cap, tok), 1).astype(F32) + 1.0
        found = []
        for c in range(2):
            rk = rank_ref[pl.ds(2 * t + c, 1), :]
            cd = code_ref[pl.ds(2 * t + c, 1), :]
            to = jnp.sum(jnp.where(rk == k, cd, 0.0), axis=1, keepdims=True)
            found.append(jnp.where(to == lane, 1.0, 0.0))
        place_ref[pl.ds(pl.multiple_of(t * slot, slot), slot), :] = jnp.concatenate(
            found, axis=0
        ).astype(BF16)

    def ring_step(k):
        ring_copy(0, k).wait_recv()
        ring_copy(1, k).wait_recv()
        if k < steps:
            ring_copy(0, k + 1).start()
            ring_copy(1, k + 1).start()
        share_copy(k).start()
        if k < steps:
            share_copy(nz - k).start()

    ring_step(1)
    w_in.wait()

    @pl.loop(0, 4)
    def _(q):
        w_rows = w_ref[pl.ds(pl.multiple_of(q * dm, dm), dm), :]
        g = dot(cot_all[z, core], w_rows, NT).astype(BF16)
        grad_ref[pl.ds(pl.multiple_of(q * mt, mt), mt), :] = g

    back_ref[...] = pair_up(dot(place_ref[...], grad_ref[...]))
    ret_ref[s] = back_ref[s]

    @pl.loop(1, spans)
    def _(i):
        back_copy(i).start()

    ring_step(2)

    def settle(h):
        @pl.loop(1, spans)
        def _(i):
            tok_copy(h, i).wait_recv()

        block = dot(place_ref[...], unpair(recv_ref[h]), TN).astype(BF16)
        for q in range(4):
            for n, c in enumerate(pieces(h)):
                merged_ref[:, q * dm + c : q * dm + c + lanes] = block[
                    q * mt : (q + 1) * mt, n * lanes : (n + 1) * lanes
                ]
        at = pl.ds(pl.multiple_of(v * width + h * lanes, lanes), lanes)
        blocks_ref[h, v] = merged_ref[:, at]

        @pl.loop(1, views)
        def _(i):
            blk_copy(h, i).start()

    settle(0)
    ring_step(3)
    settle(1)

    bias_in.wait()

    @pl.loop(0, 4)
    def _(t):
        at = pl.ds(pl.multiple_of(t * 256, 256), 256)
        o = dot(merged_ref[...], w_ref[:, at]) + bias_ref[at].astype(F32)[None, :]
        merged_out_ref[0, :, at] = o.astype(BF16)

    merged_put.start()

    ring_step(4)

    @pl.loop(0, nz)
    def _(k):
        share_copy(k).wait_recv()

    depth = views * mt

    def multiply(h):
        @pl.loop(1, views)
        def _(i):
            blk_copy(h, i).wait_recv()

        lhs = blocks_ref[h].reshape(depth, lanes)
        prod_a[h] = dot(lhs, cot_all[:, :, :, :na].reshape(depth, na), TN).reshape(
            prod_a.shape[1:]
        )

        @pl.loop(1, side)
        def _(i):
            sum_a(h, i).start()

        prod_b[h] = dot(lhs, cot_all[:, :, :, na:].reshape(depth, dm - na), TN).reshape(
            prod_b.shape[1:]
        )
        for t in range(2):

            @pl.when(x != 2 * h + t)
            def _():
                sum_b(h, t, x).start()

            @pl.when(x == 2 * h + t)
            def _():
                in_b[x] = prod_b[h, t]

        in_a[h, y] = prod_a[h, :, y]

    def combine(h):
        @pl.loop(1, side)
        def _(i):
            sum_a(h, i).wait_recv()

        part_a[h] = jnp.sum(in_a[h], axis=0)
        for t in range(2):

            @pl.when(x != 2 * h + t)
            def _():
                last_a_copy(h, t, x).start()

            @pl.when(x == 2 * h + t)
            def _():
                last_a[x] = part_a[h, t]

        @pl.when(mine_half == h)
        def _():
            @pl.loop(1, side)
            def _(i):
                sum_b(h, 0, x ^ i).wait_recv()

            part_b[...] = jnp.sum(in_b[...], axis=0)
            last_b[y] = part_b[y]

            @pl.loop(1, side)
            def _(i):
                last_b_copy(i).start()

    multiply(0)

    sums = dot(jnp.ones((8, depth), BF16), cot_all[...].reshape(depth, dm))
    for i in range(dm // 128):
        span_bias[s, i : i + 1, :] = sums[0:1, i * 128 : (i + 1) * 128]

    @pl.loop(1, spans)
    def _(i):
        bias_copy(i).start()

    multiply(1)
    combine(0)
    combine(1)

    @pl.loop(1, spans)
    def _(i):
        back_copy(i).wait_recv()

    token_grad_ref[0] = dot(pick_ref[...], unpair(ret_ref[...]), TN).astype(BF16)
    tokens_put.start()

    @pl.loop(1, spans)
    def _(i):
        bias_copy(i).wait_recv()

    bias_grad_ref[...] = jnp.sum(span_bias[...], axis=0) * scale
    bias_put.start()

    @pl.loop(1, side)
    def _(i):
        last_a_copy(0, 0, x ^ i).wait_recv()
        last_b_copy(i).wait_recv()

    weight_grad_ref[:, :na] = jnp.sum(last_a[...], axis=0) * scale
    weight_grad_ref[:, na:] = jnp.sum(last_b[...], axis=0) * scale
    weight_put.start()

    @pl.loop(1, spans)
    def _(i):
        tok_copy(0, i).wait_send()
        tok_copy(1, i).wait_send()
        back_copy(i).wait_send()
        bias_copy(i).wait_send()

    @pl.loop(1, views)
    def _(i):
        blk_copy(0, i).wait_send()
        blk_copy(1, i).wait_send()

    for k in range(1, steps + 1):
        ring_copy(0, k).wait_send()
        ring_copy(1, k).wait_send()

    @pl.loop(0, nz)
    def _(k):
        share_copy(k).wait_send()

    @pl.loop(1, side)
    def _(i):
        sum_a(0, i).wait_send()
        sum_a(1, i).wait_send()
        last_b_copy(i).wait_send()

    for h in range(2):
        for t in range(2):

            @pl.when(x != 2 * h + t)
            def _():
                sum_b(h, t, x).wait_send()
                last_a_copy(h, t, x).wait_send()

    merged_put.wait()
    tokens_put.wait()
    bias_put.wait()
    weight_put.wait()


def hand_over(*refs):
    n = (len(refs) - 1) // 2
    copies = [pltpu.make_async_copy(refs[i], refs[n + i], refs[-1].at[i]) for i in range(n)]
    for copy in copies:
        copy.start()
    for copy in copies:
        copy.wait()


def body(views, spans, tokens, scan_order, w_merge, bias, cotangent):
    tok, dm = tokens.shape[1:]
    merge_in, do = w_merge.shape
    mt = tok // 4
    half = dm // 2
    cap = 3 * (tok // spans) // 2
    slot = 2 * cap
    lanes = merge_in // views // 2
    part = merge_in // (views * spans)
    side = 4
    nz = views // 2
    na = 5 * do // 8
    nb = do - na
    scale = 1.0 / math.sqrt(views * spans * mt)
    hbm = pl.BlockSpec(memory_space=pl.ANY)
    dma = pltpu.SemaphoreType.DMA
    merged_out, token_grad, weight_grad, bias_grad = pl.pallas_call(
        functools.partial(kernel, views, spans, 128, scale),
        out_shape=(
            jax.ShapeDtypeStruct((1, mt, do), BF16),
            jax.ShapeDtypeStruct((1, tok, dm), BF16),
            jax.ShapeDtypeStruct((part, do), F32),
            jax.ShapeDtypeStruct((do // 128, 128), F32),
        ),
        in_specs=[hbm] * 5,
        out_specs=(hbm,) * 4,
        scratch_shapes=[
            pltpu.VMEM((1, mt, do), BF16),
            pltpu.VMEM((1, tok, dm), BF16),
            pltpu.VMEM((part, do), F32),
            pltpu.VMEM((do // 128, 128), F32),
            pltpu.VMEM((merge_in, do), BF16),
            pltpu.VMEM((tok, dm), BF16),
            pltpu.VMEM((1, spans * tok), jnp.int32),
            pltpu.VMEM((do,), BF16),
            pltpu.VMEM((2, spans, slot, half // 2), BF16),
            pltpu.VMEM((2, spans, slot, half // 2), BF16),
            pltpu.VMEM((spans, slot, half), BF16),
            pltpu.VMEM((spans, slot, half), BF16),
            pltpu.VMEM((spans * cap, tok), BF16),
            pltpu.VMEM((spans * cap, tok), BF16),
            pltpu.VMEM((spans, tok), F32),
            pltpu.VMEM((spans, tok), F32),
            pltpu.VMEM((mt, merge_in), BF16),
            pltpu.VMEM((tok, dm), BF16),
            pltpu.VMEM((2, views, mt, lanes), BF16),
            pltpu.VMEM((nz, 2, mt, do), BF16),
            pltpu.VMEM((2, 2, side, part, na), F32),
            pltpu.VMEM((2, 2, side, part, nb), F32),
            pltpu.VMEM((2, side, 2, part, na), F32),
            pltpu.VMEM((side, side, part, nb), F32),
            pltpu.VMEM((2, 2, part, na), F32),
            pltpu.VMEM((side, part, nb), F32),
            pltpu.VMEM((side, part, na), F32),
            pltpu.VMEM((side, part, nb), F32),
            pltpu.VMEM((spans, do // 128, 128), F32),
            dma((9,)),
            dma((2 * spans,)),
            dma((2 * spans,)),
            dma((spans,)),
            dma((spans,)),
            dma((2 * views,)),
            dma((2 * views,)),
            dma((nz + 2,)),
            dma((nz + 2,)),
            dma((nz,)),
            dma((nz,)),
            dma((spans,)),
            dma((spans,)),
            dma((2 * side,)),
            dma((2 * side,)),
            dma((side,)),
            dma((side,)),
            dma((side,)),
            dma((side,)),
            dma((side,)),
            dma((side,)),
        ],
        compiler_params=pltpu.CompilerParams(
            collective_id=0, has_side_effects=True, vmem_limit_bytes=60 * 2**20
        ),
    )(tokens, scan_order, w_merge, bias, cotangent)
    results = (merged_out, token_grad, weight_grad, bias_grad)
    merged_out, token_grad, weight_grad, bias_grad = pl.pallas_call(
        hand_over,
        out_shape=tuple(jax.ShapeDtypeStruct(r.shape, r.dtype) for r in results),
        in_specs=[hbm] * 4,
        out_specs=(hbm,) * 4,
        scratch_shapes=[dma((4,))],
    )(*results)
    return merged_out, token_grad, weight_grad, bias_grad.reshape(do)


def solution(mesh):
    in_specs = (P("view", "span", None), P("view", None), P(), P(), P("view", "span", None))
    out_specs = (P("view", "span", None), P("view", "span", None), P(("view", "span"), None), P())
    return jax.shard_map(
        functools.partial(body, mesh.shape["view"], mesh.shape["span"]),
        mesh=mesh,
        in_specs=in_specs,
        out_specs=out_specs,
        check_vma=False,
    )
```

```python
import functools
import math

import jax
import jax.numpy as jnp
from jax import lax
from jax.experimental import pallas as pl
from jax.experimental.pallas import tpu as pltpu
from jax.sharding import PartitionSpec as P

MESH = pl.DeviceIdType.MESH
F32 = jnp.float32
BF16 = jnp.bfloat16
NN = (((1,), (0,)), ((), ()))
NT = (((1,), (1,)), ((), ()))
TN = (((0,), (0,)), ((), ()))


def dot(a, b, dims=NN):
    return lax.dot_general(a, b, dims, preferred_element_type=F32)


def one_hot(hit):
    return jnp.where(hit, 1.0, 0.0).astype(BF16)


def kernel(
    views,
    spans,
    cols,
    scale,
    tokens_hbm,
    order_hbm,
    w_hbm,
    bias_hbm,
    cot_hbm,
    merged_out_hbm,
    token_grad_hbm,
    weight_grad_hbm,
    bias_grad_hbm,
    merged_out_ref,
    token_grad_ref,
    weight_grad_ref,
    bias_grad_ref,
    w_ref,
    tokens_ref,
    order_ref,
    bias_ref,
    out_ref,
    recv_ref,
    back_ref,
    ret_ref,
    pick_ref,
    place_ref,
    rank_ref,
    code_ref,
    merged_ref,
    grad_ref,
    blocks_ref,
    cot_all,
    prod_a,
    prod_b,
    in_a,
    in_b,
    part_a,
    part_b,
    last_a,
    last_b,
    span_bias,
    in_sem,
    tok_send,
    tok_recv,
    back_send,
    back_recv,
    blk_send,
    blk_recv,
    ring_send,
    ring_recv,
    share_send,
    share_recv,
    bias_send,
    bias_recv,
    sum_a_send,
    sum_a_recv,
    sum_b_send,
    sum_b_recv,
    last_a_send,
    last_a_recv,
    last_b_send,
    last_b_recv,
):
    v = lax.axis_index("view")
    s = lax.axis_index("span")
    core = lax.rem(v, 2)
    z = v // 2
    nz = views // 2
    steps = nz // 2
    side = 4
    x, y = s // side, lax.rem(s, side)
    mine_half = x // 2
    tok, dm = tokens_ref.shape
    half = dm // 2
    mt = tok // 4
    cap = 3 * (tok // spans) // 2
    slot = 2 * cap
    lanes = blocks_ref.shape[3]
    width = 2 * lanes
    na = prod_a.shape[4]

    order_in = pltpu.make_async_copy(order_hbm, order_ref, in_sem.at[0])
    tokens_in = pltpu.make_async_copy(tokens_hbm.at[0], tokens_ref, in_sem.at[1])
    cot_in = pltpu.make_async_copy(cot_hbm.at[0], cot_all.at[z, core], in_sem.at[2])
    w_in = pltpu.make_async_copy(w_hbm, w_ref, in_sem.at[3])
    bias_in = pltpu.make_async_copy(bias_hbm, bias_ref, in_sem.at[4])
    merged_put = pltpu.make_async_copy(merged_out_ref, merged_out_hbm, in_sem.at[5])
    tokens_put = pltpu.make_async_copy(token_grad_ref, token_grad_hbm, in_sem.at[6])
    weight_put = pltpu.make_async_copy(weight_grad_ref, weight_grad_hbm, in_sem.at[7])
    bias_put = pltpu.make_async_copy(bias_grad_ref, bias_grad_hbm, in_sem.at[8])
    order_in.start()
    tokens_in.start()
    cot_in.start()

    barrier = pltpu.get_barrier_semaphore()

    @pl.loop(1, spans)
    def _(i):
        pl.semaphore_signal(barrier, inc=1, device_id=(v, s ^ i), device_id_type=MESH)

    @pl.loop(1, views)
    def _(i):
        pl.semaphore_signal(barrier, inc=1, device_id=(v ^ i, s), device_id_type=MESH)

    w_in.start()
    bias_in.start()

    def remote(src, dst, send, recv, device):
        return pltpu.make_async_remote_copy(
            src_ref=src,
            dst_ref=dst,
            send_sem=send,
            recv_sem=recv,
            device_id=device,
            device_id_type=MESH,
        )

    def tok_copy(h, i):
        at = h * spans + i
        return remote(
            out_ref.at[h, s ^ i], recv_ref.at[h, s], tok_send.at[at], tok_recv.at[at], (v, s ^ i)
        )

    def back_copy(i):
        return remote(
            back_ref.at[s ^ i], ret_ref.at[s], back_send.at[i], back_recv.at[i], (v, s ^ i)
        )

    def blk_copy(h, i):
        d = v ^ i
        at = h * views + i
        src = merged_ref.at[:, pl.ds(pl.multiple_of(d * width + h * lanes, lanes), lanes)]
        return remote(src, blocks_ref.at[h, v], blk_send.at[at], blk_recv.at[at], (d, s))

    def near(k):
        return lax.rem(z + 2 * nz - k, nz)

    def ring_copy(way, k):
        held = near(k - 1) if way == 0 else near(1 - k)
        to = near(-1) if way == 0 else near(1)
        ref = cot_all.at[held, core]
        if k == steps:
            ref = ref.at[:, way * half : (way + 1) * half]
        at = way * (steps + 1) + k
        return remote(ref, ref, ring_send.at[at], ring_recv.at[at], (to * 2 + core, s))

    def share_copy(k):
        ref = cot_all.at[near(k), core]
        return remote(ref, ref, share_send.at[k], share_recv.at[k], (v ^ 1, s))

    def bias_copy(i):
        ref = span_bias.at[s]
        return remote(ref, ref, bias_send.at[i], bias_recv.at[i], (v, s ^ i))

    def sum_a(h, i):
        at = h * side + i
        return remote(
            prod_a.at[h, :, y ^ i], in_a.at[h, y], sum_a_send.at[at], sum_a_recv.at[at], (v, s ^ i)
        )

    def sum_b(h, t, k):
        to = (2 * h + t) * side + y
        return remote(
            prod_b.at[h, t], in_b.at[k], sum_b_send.at[2 * h + t], sum_b_recv.at[k], (v, to)
        )

    def last_a_copy(h, t, k):
        to = (2 * h + t) * side + y
        return remote(
            part_a.at[h, t], last_a.at[k], last_a_send.at[2 * h + t], last_a_recv.at[k], (v, to)
        )

    def last_b_copy(i):
        return remote(
            part_b.at[y ^ i], last_b.at[y], last_b_send.at[i], last_b_recv.at[i], (v, s ^ i)
        )

    def pair_up(rows):
        n = rows.shape[1] // 2
        a = rows[:, :n].reshape(spans, cap, n)
        b = rows[:, n:].reshape(spans, cap, n)
        return jnp.concatenate([a, b], axis=1).astype(BF16)

    def unpair(slots):
        wide = slots.astype(F32)
        n = wide.shape[2]
        a = wide[:, :cap].reshape(spans * cap, n)
        b = wide[:, cap:].reshape(spans * cap, n)
        return jnp.concatenate([a, b], axis=1).astype(BF16)

    before = one_hot(
        lax.broadcasted_iota(jnp.int32, (tok, tok), 0)
        < lax.broadcasted_iota(jnp.int32, (tok, tok), 1)
    )
    bits = int(math.log2(tok))
    order_in.wait()
    mine = order_ref[0:1, pl.ds(pl.multiple_of(s * tok, tok), tok)]
    owner = lax.shift_right_logical(mine, bits)
    hot = jnp.where(lax.broadcasted_iota(jnp.int32, (spans, tok), 0) == owner, 1.0, 0.0)
    rank = jnp.sum(dot(hot.astype(BF16), before) * hot, axis=0, keepdims=True).astype(jnp.int32)
    to_slot = owner * cap + rank
    pick_ref[...] = one_hot(lax.broadcasted_iota(jnp.int32, (spans * cap, tok), 0) == to_slot)
    tokens_in.wait()

    def pieces(h):
        return [c + h * lanes for c in range(0, dm, width)]

    def fill(h):
        part = jnp.concatenate([tokens_ref[:, c : c + lanes] for c in pieces(h)], axis=1)
        out_ref[h] = pair_up(dot(pick_ref[...], part))
        recv_ref[h, s] = out_ref[h, s]

    fill(0)
    cot_in.wait()
    pl.semaphore_wait(barrier, spans + views - 2)
    ring_copy(0, 1).start()
    ring_copy(1, 1).start()

    @pl.loop(1, spans)
    def _(i):
        tok_copy(0, i).start()

    share_copy(0).start()
    fill(1)

    @pl.loop(1, spans)
    def _(i):
        tok_copy(1, i).start()

    order = jnp.concatenate([order_ref[0:1, c * tok : (c + 1) * tok] for c in range(spans)], axis=0)
    arriving = lax.shift_right_logical(order, bits) == s
    arrive = jnp.where(arriving, 1.0, 0.0)
    rank_in = dot(arrive.astype(BF16), before)
    rank_ref[...] = jnp.where(arriving, rank_in, -1.0)
    local = lax.rem(order, tok)
    col = lax.rem(local, cols)
    quadrant = (local // cols) * 2 + lax.rem(col, 2)
    code_ref[...] = jnp.where(arriving, quadrant * mt + col // 2 + 1, 0).astype(F32)

    @pl.loop(0, spans // 2)
    def _(t):
        k = lax.broadcasted_iota(jnp.int32, (cap, tok), 0).astype(F32)
        lane = lax.broadcasted_iota(jnp.int32, (cap, tok), 1).astype(F32) + 1.0
        found = []
        for c in range(2):
            rk = rank_ref[pl.ds(2 * t + c, 1), :]
            cd = code_ref[pl.ds(2 * t + c, 1), :]
            to = jnp.sum(jnp.where(rk == k, cd, 0.0), axis=1, keepdims=True)
            found.append(jnp.where(to == lane, 1.0, 0.0))
        place_ref[pl.ds(pl.multiple_of(t * slot, slot), slot), :] = jnp.concatenate(
            found, axis=0
        ).astype(BF16)

    def ring_step(k):
        ring_copy(0, k).wait_recv()
        ring_copy(1, k).wait_recv()
        if k < steps:
            ring_copy(0, k + 1).start()
            ring_copy(1, k + 1).start()
        share_copy(k).start()
        if k < steps:
            share_copy(nz - k).start()

    ring_step(1)
    w_in.wait()

    @pl.loop(0, 4)
    def _(q):
        w_rows = w_ref[pl.ds(pl.multiple_of(q * dm, dm), dm), :]
        g = dot(cot_all[z, core], w_rows, NT).astype(BF16)
        grad_ref[pl.ds(pl.multiple_of(q * mt, mt), mt), :] = g

    back_ref[...] = pair_up(dot(place_ref[...], grad_ref[...]))
    ret_ref[s] = back_ref[s]

    @pl.loop(1, spans)
    def _(i):
        back_copy(i).start()

    ring_step(2)

    def settle(h):
        @pl.loop(1, spans)
        def _(i):
            tok_copy(h, i).wait_recv()

        block = dot(place_ref[...], unpair(recv_ref[h]), TN).astype(BF16)
        for q in range(4):
            for n, c in enumerate(pieces(h)):
                merged_ref[:, q * dm + c : q * dm + c + lanes] = block[
                    q * mt : (q + 1) * mt, n * lanes : (n + 1) * lanes
                ]
        at = pl.ds(pl.multiple_of(v * width + h * lanes, lanes), lanes)
        blocks_ref[h, v] = merged_ref[:, at]

        @pl.loop(1, views)
        def _(i):
            blk_copy(h, i).start()

    settle(0)
    ring_step(3)
    settle(1)

    bias_in.wait()

    @pl.loop(0, 4)
    def _(t):
        at = pl.ds(pl.multiple_of(t * 256, 256), 256)
        o = dot(merged_ref[...], w_ref[:, at]) + bias_ref[at].astype(F32)[None, :]
        merged_out_ref[0, :, at] = o.astype(BF16)

    merged_put.start()

    ring_step(4)

    @pl.loop(0, nz)
    def _(k):
        share_copy(k).wait_recv()

    depth = views * mt

    def multiply(h):
        @pl.loop(1, views)
        def _(i):
            blk_copy(h, i).wait_recv()

        lhs = blocks_ref[h].reshape(depth, lanes)
        prod_a[h] = dot(lhs, cot_all[:, :, :, :na].reshape(depth, na), TN).reshape(
            prod_a.shape[1:]
        )

        @pl.loop(1, side)
        def _(i):
            sum_a(h, i).start()

        prod_b[h] = dot(lhs, cot_all[:, :, :, na:].reshape(depth, dm - na), TN).reshape(
            prod_b.shape[1:]
        )
        for t in range(2):

            @pl.when(x != 2 * h + t)
            def _():
                sum_b(h, t, x).start()

            @pl.when(x == 2 * h + t)
            def _():
                in_b[x] = prod_b[h, t]

        in_a[h, y] = prod_a[h, :, y]

    def combine(h):
        @pl.loop(1, side)
        def _(i):
            sum_a(h, i).wait_recv()

        part_a[h] = jnp.sum(in_a[h], axis=0)
        for t in range(2):

            @pl.when(x != 2 * h + t)
            def _():
                last_a_copy(h, t, x).start()

            @pl.when(x == 2 * h + t)
            def _():
                last_a[x] = part_a[h, t]

        @pl.when(mine_half == h)
        def _():
            @pl.loop(1, side)
            def _(i):
                sum_b(h, 0, x ^ i).wait_recv()

            part_b[...] = jnp.sum(in_b[...], axis=0)
            last_b[y] = part_b[y]

            @pl.loop(1, side)
            def _(i):
                last_b_copy(i).start()

    multiply(0)

    sums = dot(jnp.ones((8, depth), BF16), cot_all[...].reshape(depth, dm))
    for i in range(dm // 128):
        span_bias[s, i : i + 1, :] = sums[0:1, i * 128 : (i + 1) * 128]

    @pl.loop(1, spans)
    def _(i):
        bias_copy(i).start()

    multiply(1)
    combine(0)
    combine(1)

    @pl.loop(1, spans)
    def _(i):
        back_copy(i).wait_recv()

    token_grad_ref[0] = dot(pick_ref[...], unpair(ret_ref[...]), TN).astype(BF16)
    tokens_put.start()

    @pl.loop(1, spans)
    def _(i):
        bias_copy(i).wait_recv()

    bias_grad_ref[...] = jnp.sum(span_bias[...], axis=0) * scale
    bias_put.start()

    @pl.loop(1, side)
    def _(i):
        last_a_copy(0, 0, x ^ i).wait_recv()
        last_b_copy(i).wait_recv()

    weight_grad_ref[:, :na] = jnp.sum(last_a[...], axis=0) * scale
    weight_grad_ref[:, na:] = jnp.sum(last_b[...], axis=0) * scale
    weight_put.start()

    @pl.loop(1, spans)
    def _(i):
        tok_copy(0, i).wait_send()
        tok_copy(1, i).wait_send()
        back_copy(i).wait_send()
        bias_copy(i).wait_send()

    @pl.loop(1, views)
    def _(i):
        blk_copy(0, i).wait_send()
        blk_copy(1, i).wait_send()

    for k in range(1, steps + 1):
        ring_copy(0, k).wait_send()
        ring_copy(1, k).wait_send()

    @pl.loop(0, nz)
    def _(k):
        share_copy(k).wait_send()

    @pl.loop(1, side)
    def _(i):
        sum_a(0, i).wait_send()
        sum_a(1, i).wait_send()
        last_b_copy(i).wait_send()

    for h in range(2):
        for t in range(2):

            @pl.when(x != 2 * h + t)
            def _():
                sum_b(h, t, x).wait_send()
                last_a_copy(h, t, x).wait_send()

    merged_put.wait()
    tokens_put.wait()
    bias_put.wait()
    weight_put.wait()


def hand_over(*refs):
    n = (len(refs) - 1) // 3
    sems = refs[-1]
    ins = [pltpu.make_async_copy(refs[i], refs[2 * n + i], sems.at[i]) for i in range(n)]
    outs = [pltpu.make_async_copy(refs[2 * n + i], refs[n + i], sems.at[n + i]) for i in range(n)]
    for copy in ins:
        copy.start()
    for read, write in zip(ins, outs):
        read.wait()
        write.start()
    for copy in outs:
        copy.wait()


def body(views, spans, tokens, scan_order, w_merge, bias, cotangent):
    tok, dm = tokens.shape[1:]
    merge_in, do = w_merge.shape
    mt = tok // 4
    half = dm // 2
    cap = 3 * (tok // spans) // 2
    slot = 2 * cap
    lanes = merge_in // views // 2
    part = merge_in // (views * spans)
    side = 4
    nz = views // 2
    na = 5 * do // 8
    nb = do - na
    scale = 1.0 / math.sqrt(views * spans * mt)
    hbm = pl.BlockSpec(memory_space=pl.ANY)
    dma = pltpu.SemaphoreType.DMA
    merged_out, token_grad, weight_grad, bias_grad = pl.pallas_call(
        functools.partial(kernel, views, spans, 128, scale),
        out_shape=(
            jax.ShapeDtypeStruct((1, mt, do), BF16),
            jax.ShapeDtypeStruct((1, tok, dm), BF16),
            jax.ShapeDtypeStruct((part, do), F32),
            jax.ShapeDtypeStruct((do // 128, 128), F32),
        ),
        in_specs=[hbm] * 5,
        out_specs=(hbm,) * 4,
        scratch_shapes=[
            pltpu.VMEM((1, mt, do), BF16),
            pltpu.VMEM((1, tok, dm), BF16),
            pltpu.VMEM((part, do), F32),
            pltpu.VMEM((do // 128, 128), F32),
            pltpu.VMEM((merge_in, do), BF16),
            pltpu.VMEM((tok, dm), BF16),
            pltpu.VMEM((1, spans * tok), jnp.int32),
            pltpu.VMEM((do,), BF16),
            pltpu.VMEM((2, spans, slot, half // 2), BF16),
            pltpu.VMEM((2, spans, slot, half // 2), BF16),
            pltpu.VMEM((spans, slot, half), BF16),
            pltpu.VMEM((spans, slot, half), BF16),
            pltpu.VMEM((spans * cap, tok), BF16),
            pltpu.VMEM((spans * cap, tok), BF16),
            pltpu.VMEM((spans, tok), F32),
            pltpu.VMEM((spans, tok), F32),
            pltpu.VMEM((mt, merge_in), BF16),
            pltpu.VMEM((tok, dm), BF16),
            pltpu.VMEM((2, views, mt, lanes), BF16),
            pltpu.VMEM((nz, 2, mt, do), BF16),
            pltpu.VMEM((2, 2, side, part, na), F32),
            pltpu.VMEM((2, 2, side, part, nb), F32),
            pltpu.VMEM((2, side, 2, part, na), F32),
            pltpu.VMEM((side, side, part, nb), F32),
            pltpu.VMEM((2, 2, part, na), F32),
            pltpu.VMEM((side, part, nb), F32),
            pltpu.VMEM((side, part, na), F32),
            pltpu.VMEM((side, part, nb), F32),
            pltpu.VMEM((spans, do // 128, 128), F32),
            dma((9,)),
            dma((2 * spans,)),
            dma((2 * spans,)),
            dma((spans,)),
            dma((spans,)),
            dma((2 * views,)),
            dma((2 * views,)),
            dma((nz + 2,)),
            dma((nz + 2,)),
            dma((nz,)),
            dma((nz,)),
            dma((spans,)),
            dma((spans,)),
            dma((2 * side,)),
            dma((2 * side,)),
            dma((side,)),
            dma((side,)),
            dma((side,)),
            dma((side,)),
            dma((side,)),
            dma((side,)),
        ],
        compiler_params=pltpu.CompilerParams(
            collective_id=0, has_side_effects=True, vmem_limit_bytes=60 * 2**20
        ),
    )(tokens, scan_order, w_merge, bias, cotangent)
    results = (merged_out, token_grad, weight_grad, bias_grad)
    merged_out, token_grad, weight_grad, bias_grad = pl.pallas_call(
        hand_over,
        out_shape=tuple(jax.ShapeDtypeStruct(r.shape, r.dtype) for r in results),
        in_specs=[hbm] * 4,
        out_specs=(hbm,) * 4,
        scratch_shapes=[pltpu.VMEM(r.shape, r.dtype) for r in results] + [dma((8,))],
    )(*results)
    return merged_out, token_grad, weight_grad, bias_grad.reshape(do)


def solution(mesh):
    in_specs = (P("view", "span", None), P("view", None), P(), P(), P("view", "span", None))
    out_specs = (P("view", "span", None), P("view", "span", None), P(("view", "span"), None), P())
    return jax.shard_map(
        functools.partial(body, mesh.shape["view"], mesh.shape["span"]),
        mesh=mesh,
        in_specs=in_specs,
        out_specs=out_specs,
        check_vma=False,
    )
```

```python
import functools
import math

import jax
import jax.numpy as jnp
from jax import lax
from jax.experimental import pallas as pl
from jax.experimental.pallas import tpu as pltpu
from jax.sharding import PartitionSpec as P

MESH = pl.DeviceIdType.MESH
F32 = jnp.float32
BF16 = jnp.bfloat16
NN = (((1,), (0,)), ((), ()))
NT = (((1,), (1,)), ((), ()))
TN = (((0,), (0,)), ((), ()))


def dot(a, b, dims=NN):
    return lax.dot_general(a, b, dims, preferred_element_type=F32)


def one_hot(hit):
    return jnp.where(hit, 1.0, 0.0).astype(BF16)


def kernel(
    views,
    spans,
    cols,
    scale,
    tokens_hbm,
    order_hbm,
    w_hbm,
    bias_hbm,
    cot_hbm,
    merged_out_hbm,
    token_grad_hbm,
    weight_grad_hbm,
    bias_grad_hbm,
    merged_out_ref,
    token_grad_ref,
    weight_grad_ref,
    bias_grad_ref,
    w_ref,
    tokens_ref,
    order_ref,
    bias_ref,
    out_ref,
    recv_ref,
    back_ref,
    ret_ref,
    pick_ref,
    place_ref,
    rank_ref,
    code_ref,
    merged_ref,
    grad_ref,
    blocks_ref,
    cot_all,
    prod_a,
    prod_b,
    in_a,
    in_b,
    part_a,
    part_b,
    last_a,
    last_b,
    span_bias,
    in_sem,
    tok_send,
    tok_recv,
    back_send,
    back_recv,
    blk_send,
    blk_recv,
    ring_send,
    ring_recv,
    share_send,
    share_recv,
    bias_send,
    bias_recv,
    sum_a_send,
    sum_a_recv,
    sum_b_send,
    sum_b_recv,
    last_a_send,
    last_a_recv,
    last_b_send,
    last_b_recv,
):
    v = lax.axis_index("view")
    s = lax.axis_index("span")
    core = lax.rem(v, 2)
    z = v // 2
    nz = views // 2
    steps = nz // 2
    side = 4
    x, y = s // side, lax.rem(s, side)
    mine_half = x // 2
    tok, dm = tokens_ref.shape
    half = dm // 2
    mt = tok // 4
    cap = 3 * (tok // spans) // 2
    slot = 2 * cap
    lanes = blocks_ref.shape[3]
    width = 2 * lanes
    na = prod_a.shape[4]

    order_in = pltpu.make_async_copy(order_hbm, order_ref, in_sem.at[0])
    tokens_in = pltpu.make_async_copy(tokens_hbm.at[0], tokens_ref, in_sem.at[1])
    cot_in = pltpu.make_async_copy(cot_hbm.at[0], cot_all.at[z, core], in_sem.at[2])
    w_in = pltpu.make_async_copy(w_hbm, w_ref, in_sem.at[3])
    bias_in = pltpu.make_async_copy(bias_hbm, bias_ref, in_sem.at[4])
    merged_put = pltpu.make_async_copy(merged_out_ref, merged_out_hbm, in_sem.at[5])
    tokens_put = pltpu.make_async_copy(token_grad_ref, token_grad_hbm, in_sem.at[6])
    weight_put = pltpu.make_async_copy(weight_grad_ref, weight_grad_hbm, in_sem.at[7])
    bias_put = pltpu.make_async_copy(bias_grad_ref, bias_grad_hbm, in_sem.at[8])
    order_in.start()
    tokens_in.start()
    cot_in.start()

    barrier = pltpu.get_barrier_semaphore()

    @pl.loop(1, spans)
    def _(i):
        pl.semaphore_signal(barrier, inc=1, device_id=(v, s ^ i), device_id_type=MESH)

    @pl.loop(1, views)
    def _(i):
        pl.semaphore_signal(barrier, inc=1, device_id=(v ^ i, s), device_id_type=MESH)

    w_in.start()
    bias_in.start()

    def remote(src, dst, send, recv, device):
        return pltpu.make_async_remote_copy(
            src_ref=src,
            dst_ref=dst,
            send_sem=send,
            recv_sem=recv,
            device_id=device,
            device_id_type=MESH,
        )

    def tok_copy(h, i):
        at = h * spans + i
        return remote(
            out_ref.at[h, s ^ i], recv_ref.at[h, s], tok_send.at[at], tok_recv.at[at], (v, s ^ i)
        )

    def back_copy(i):
        return remote(
            back_ref.at[s ^ i], ret_ref.at[s], back_send.at[i], back_recv.at[i], (v, s ^ i)
        )

    def blk_copy(h, i):
        d = v ^ i
        at = h * views + i
        src = merged_ref.at[:, pl.ds(pl.multiple_of(d * width + h * lanes, lanes), lanes)]
        return remote(src, blocks_ref.at[h, v], blk_send.at[at], blk_recv.at[at], (d, s))

    def near(k):
        return lax.rem(z + 2 * nz - k, nz)

    def ring_copy(way, k):
        held = near(k - 1) if way == 0 else near(1 - k)
        to = near(-1) if way == 0 else near(1)
        ref = cot_all.at[held, core]
        if k == steps:
            ref = ref.at[:, way * half : (way + 1) * half]
        at = way * (steps + 1) + k
        return remote(ref, ref, ring_send.at[at], ring_recv.at[at], (to * 2 + core, s))

    def share_copy(k):
        ref = cot_all.at[near(k), core]
        return remote(ref, ref, share_send.at[k], share_recv.at[k], (v ^ 1, s))

    def bias_copy(i):
        ref = span_bias.at[s]
        return remote(ref, ref, bias_send.at[i], bias_recv.at[i], (v, s ^ i))

    def sum_a(h, i):
        at = h * side + i
        return remote(
            prod_a.at[h, :, y ^ i], in_a.at[h, y], sum_a_send.at[at], sum_a_recv.at[at], (v, s ^ i)
        )

    def sum_b(h, t, k):
        to = (2 * h + t) * side + y
        return remote(
            prod_b.at[h, t], in_b.at[k], sum_b_send.at[2 * h + t], sum_b_recv.at[k], (v, to)
        )

    def last_a_copy(h, t, k):
        to = (2 * h + t) * side + y
        return remote(
            part_a.at[h, t], last_a.at[k], last_a_send.at[2 * h + t], last_a_recv.at[k], (v, to)
        )

    def last_b_copy(i):
        return remote(
            part_b.at[y ^ i], last_b.at[y], last_b_send.at[i], last_b_recv.at[i], (v, s ^ i)
        )

    def pair_up(rows):
        n = rows.shape[1] // 2
        a = rows[:, :n].reshape(spans, cap, n)
        b = rows[:, n:].reshape(spans, cap, n)
        return jnp.concatenate([a, b], axis=1).astype(BF16)

    def unpair(slots):
        wide = slots.astype(F32)
        n = wide.shape[2]
        a = wide[:, :cap].reshape(spans * cap, n)
        b = wide[:, cap:].reshape(spans * cap, n)
        return jnp.concatenate([a, b], axis=1).astype(BF16)

    before = one_hot(
        lax.broadcasted_iota(jnp.int32, (tok, tok), 0)
        < lax.broadcasted_iota(jnp.int32, (tok, tok), 1)
    )
    bits = int(math.log2(tok))
    order_in.wait()
    mine = order_ref[0:1, pl.ds(pl.multiple_of(s * tok, tok), tok)]
    owner = lax.shift_right_logical(mine, bits)
    hot = jnp.where(lax.broadcasted_iota(jnp.int32, (spans, tok), 0) == owner, 1.0, 0.0)
    rank = jnp.sum(dot(hot.astype(BF16), before) * hot, axis=0, keepdims=True).astype(jnp.int32)
    to_slot = owner * cap + rank
    pick_ref[...] = one_hot(lax.broadcasted_iota(jnp.int32, (spans * cap, tok), 0) == to_slot)
    tokens_in.wait()

    def pieces(h):
        return [c + h * lanes for c in range(0, dm, width)]

    def fill(h):
        part = jnp.concatenate([tokens_ref[:, c : c + lanes] for c in pieces(h)], axis=1)
        out_ref[h] = pair_up(dot(pick_ref[...], part))
        recv_ref[h, s] = out_ref[h, s]

    fill(0)
    cot_in.wait()
    pl.semaphore_wait(barrier, spans + views - 2)
    ring_copy(0, 1).start()
    ring_copy(1, 1).start()

    @pl.loop(1, spans)
    def _(i):
        tok_copy(0, i).start()

    share_copy(0).start()
    fill(1)

    @pl.loop(1, spans)
    def _(i):
        tok_copy(1, i).start()

    order = jnp.concatenate([order_ref[0:1, c * tok : (c + 1) * tok] for c in range(spans)], axis=0)
    arriving = lax.shift_right_logical(order, bits) == s
    arrive = jnp.where(arriving, 1.0, 0.0)
    rank_in = dot(arrive.astype(BF16), before)
    rank_ref[...] = jnp.where(arriving, rank_in, -1.0)
    local = lax.rem(order, tok)
    col = lax.rem(local, cols)
    quadrant = (local // cols) * 2 + lax.rem(col, 2)
    code_ref[...] = jnp.where(arriving, quadrant * mt + col // 2 + 1, 0).astype(F32)

    @pl.loop(0, spans // 2)
    def _(t):
        k = lax.broadcasted_iota(jnp.int32, (cap, tok), 0).astype(F32)
        lane = lax.broadcasted_iota(jnp.int32, (cap, tok), 1).astype(F32) + 1.0
        found = []
        for c in range(2):
            rk = rank_ref[pl.ds(2 * t + c, 1), :]
            cd = code_ref[pl.ds(2 * t + c, 1), :]
            to = jnp.sum(jnp.where(rk == k, cd, 0.0), axis=1, keepdims=True)
            found.append(jnp.where(to == lane, 1.0, 0.0))
        place_ref[pl.ds(pl.multiple_of(t * slot, slot), slot), :] = jnp.concatenate(
            found, axis=0
        ).astype(BF16)

    def ring_step(k):
        ring_copy(0, k).wait_recv()
        ring_copy(1, k).wait_recv()
        if k < steps:
            ring_copy(0, k + 1).start()
            ring_copy(1, k + 1).start()
        share_copy(k).start()
        if k < steps:
            share_copy(nz - k).start()

    ring_step(1)
    w_in.wait()

    @pl.loop(0, 4)
    def _(q):
        w_rows = w_ref[pl.ds(pl.multiple_of(q * dm, dm), dm), :]
        g = dot(cot_all[z, core], w_rows, NT).astype(BF16)
        grad_ref[pl.ds(pl.multiple_of(q * mt, mt), mt), :] = g

    back_ref[...] = pair_up(dot(place_ref[...], grad_ref[...]))
    ret_ref[s] = back_ref[s]

    @pl.loop(1, spans)
    def _(i):
        back_copy(i).start()

    ring_step(2)

    def settle(h):
        @pl.loop(1, spans)
        def _(i):
            tok_copy(h, i).wait_recv()

        block = dot(place_ref[...], unpair(recv_ref[h]), TN).astype(BF16)
        for q in range(4):
            for n, c in enumerate(pieces(h)):
                merged_ref[:, q * dm + c : q * dm + c + lanes] = block[
                    q * mt : (q + 1) * mt, n * lanes : (n + 1) * lanes
                ]
        at = pl.ds(pl.multiple_of(v * width + h * lanes, lanes), lanes)
        blocks_ref[h, v] = merged_ref[:, at]

        @pl.loop(1, views)
        def _(i):
            blk_copy(h, i).start()

    settle(0)
    ring_step(3)
    settle(1)

    ring_step(4)

    @pl.loop(0, nz)
    def _(k):
        share_copy(k).wait_recv()

    depth = views * mt

    def multiply(h):
        @pl.loop(1, views)
        def _(i):
            blk_copy(h, i).wait_recv()

        lhs = blocks_ref[h].reshape(depth, lanes)
        prod_a[h] = dot(lhs, cot_all[:, :, :, :na].reshape(depth, na), TN).reshape(
            prod_a.shape[1:]
        )

        @pl.loop(1, side)
        def _(i):
            sum_a(h, i).start()

        prod_b[h] = dot(lhs, cot_all[:, :, :, na:].reshape(depth, dm - na), TN).reshape(
            prod_b.shape[1:]
        )
        for t in range(2):

            @pl.when(x != 2 * h + t)
            def _():
                sum_b(h, t, x).start()

            @pl.when(x == 2 * h + t)
            def _():
                in_b[x] = prod_b[h, t]

        in_a[h, y] = prod_a[h, :, y]

    def combine(h):
        @pl.loop(1, side)
        def _(i):
            sum_a(h, i).wait_recv()

        part_a[h] = jnp.sum(in_a[h], axis=0)
        for t in range(2):

            @pl.when(x != 2 * h + t)
            def _():
                last_a_copy(h, t, x).start()

            @pl.when(x == 2 * h + t)
            def _():
                last_a[x] = part_a[h, t]

        @pl.when(mine_half == h)
        def _():
            @pl.loop(1, side)
            def _(i):
                sum_b(h, 0, x ^ i).wait_recv()

            part_b[...] = jnp.sum(in_b[...], axis=0)
            last_b[y] = part_b[y]

            @pl.loop(1, side)
            def _(i):
                last_b_copy(i).start()

    multiply(0)
    multiply(1)

    bias_in.wait()

    @pl.loop(0, 4)
    def _(t):
        at = pl.ds(pl.multiple_of(t * 256, 256), 256)
        o = dot(merged_ref[...], w_ref[:, at]) + bias_ref[at].astype(F32)[None, :]
        merged_out_ref[0, :, at] = o.astype(BF16)

    merged_put.start()

    sums = dot(jnp.ones((8, depth), BF16), cot_all[...].reshape(depth, dm))
    for i in range(dm // 128):
        span_bias[s, i : i + 1, :] = sums[0:1, i * 128 : (i + 1) * 128]

    @pl.loop(1, spans)
    def _(i):
        bias_copy(i).start()

    @pl.loop(1, spans)
    def _(i):
        tok_copy(0, i).wait_send()
        tok_copy(1, i).wait_send()
        back_copy(i).wait_send()

    @pl.loop(1, views)
    def _(i):
        blk_copy(0, i).wait_send()
        blk_copy(1, i).wait_send()

    for k in range(1, steps + 1):
        ring_copy(0, k).wait_send()
        ring_copy(1, k).wait_send()

    @pl.loop(0, nz)
    def _(k):
        share_copy(k).wait_send()

    combine(0)
    combine(1)

    @pl.loop(1, spans)
    def _(i):
        back_copy(i).wait_recv()

    token_grad_ref[0] = dot(pick_ref[...], unpair(ret_ref[...]), TN).astype(BF16)
    tokens_put.start()

    @pl.loop(1, spans)
    def _(i):
        bias_copy(i).wait_recv()

    bias_grad_ref[...] = jnp.sum(span_bias[...], axis=0) * scale
    bias_put.start()

    @pl.loop(1, spans)
    def _(i):
        bias_copy(i).wait_send()

    @pl.loop(1, side)
    def _(i):
        sum_a(0, i).wait_send()
        sum_a(1, i).wait_send()

    @pl.loop(1, side)
    def _(i):
        last_a_copy(0, 0, x ^ i).wait_recv()
        last_b_copy(i).wait_recv()

    weight_grad_ref[:, :na] = jnp.sum(last_a[...], axis=0) * scale
    weight_grad_ref[:, na:] = jnp.sum(last_b[...], axis=0) * scale
    weight_put.start()

    @pl.loop(1, side)
    def _(i):
        last_b_copy(i).wait_send()

    for h in range(2):
        for t in range(2):

            @pl.when(x != 2 * h + t)
            def _():
                sum_b(h, t, x).wait_send()
                last_a_copy(h, t, x).wait_send()

    merged_put.wait()
    tokens_put.wait()
    bias_put.wait()
    weight_put.wait()


def hand_over(*refs):
    n = (len(refs) - 1) // 3
    sems = refs[-1]
    ins = [pltpu.make_async_copy(refs[i], refs[2 * n + i], sems.at[i]) for i in range(n)]
    outs = [pltpu.make_async_copy(refs[2 * n + i], refs[n + i], sems.at[n + i]) for i in range(n)]
    for copy in ins:
        copy.start()
    for read, write in zip(ins, outs):
        read.wait()
        write.start()
    for copy in outs:
        copy.wait()


def body(views, spans, tokens, scan_order, w_merge, bias, cotangent):
    tok, dm = tokens.shape[1:]
    merge_in, do = w_merge.shape
    mt = tok // 4
    half = dm // 2
    cap = 3 * (tok // spans) // 2
    slot = 2 * cap
    lanes = merge_in // views // 2
    part = merge_in // (views * spans)
    side = 4
    nz = views // 2
    na = 5 * do // 8
    nb = do - na
    scale = 1.0 / math.sqrt(views * spans * mt)
    hbm = pl.BlockSpec(memory_space=pl.ANY)
    dma = pltpu.SemaphoreType.DMA
    merged_out, token_grad, weight_grad, bias_grad = pl.pallas_call(
        functools.partial(kernel, views, spans, 128, scale),
        out_shape=(
            jax.ShapeDtypeStruct((1, mt, do), BF16),
            jax.ShapeDtypeStruct((1, tok, dm), BF16),
            jax.ShapeDtypeStruct((part, do), F32),
            jax.ShapeDtypeStruct((do // 128, 128), F32),
        ),
        in_specs=[hbm] * 5,
        out_specs=(hbm,) * 4,
        scratch_shapes=[
            pltpu.VMEM((1, mt, do), BF16),
            pltpu.VMEM((1, tok, dm), BF16),
            pltpu.VMEM((part, do), F32),
            pltpu.VMEM((do // 128, 128), F32),
            pltpu.VMEM((merge_in, do), BF16),
            pltpu.VMEM((tok, dm), BF16),
            pltpu.VMEM((1, spans * tok), jnp.int32),
            pltpu.VMEM((do,), BF16),
            pltpu.VMEM((2, spans, slot, half // 2), BF16),
            pltpu.VMEM((2, spans, slot, half // 2), BF16),
            pltpu.VMEM((spans, slot, half), BF16),
            pltpu.VMEM((spans, slot, half), BF16),
            pltpu.VMEM((spans * cap, tok), BF16),
            pltpu.VMEM((spans * cap, tok), BF16),
            pltpu.VMEM((spans, tok), F32),
            pltpu.VMEM((spans, tok), F32),
            pltpu.VMEM((mt, merge_in), BF16),
            pltpu.VMEM((tok, dm), BF16),
            pltpu.VMEM((2, views, mt, lanes), BF16),
            pltpu.VMEM((nz, 2, mt, do), BF16),
            pltpu.VMEM((2, 2, side, part, na), F32),
            pltpu.VMEM((2, 2, side, part, nb), F32),
            pltpu.VMEM((2, side, 2, part, na), F32),
            pltpu.VMEM((side, side, part, nb), F32),
            pltpu.VMEM((2, 2, part, na), F32),
            pltpu.VMEM((side, part, nb), F32),
            pltpu.VMEM((side, part, na), F32),
            pltpu.VMEM((side, part, nb), F32),
            pltpu.VMEM((spans, do // 128, 128), F32),
            dma((9,)),
            dma((2 * spans,)),
            dma((2 * spans,)),
            dma((spans,)),
            dma((spans,)),
            dma((2 * views,)),
            dma((2 * views,)),
            dma((nz + 2,)),
            dma((nz + 2,)),
            dma((nz,)),
            dma((nz,)),
            dma((spans,)),
            dma((spans,)),
            dma((2 * side,)),
            dma((2 * side,)),
            dma((side,)),
            dma((side,)),
            dma((side,)),
            dma((side,)),
            dma((side,)),
            dma((side,)),
        ],
        compiler_params=pltpu.CompilerParams(
            collective_id=0, has_side_effects=True, vmem_limit_bytes=60 * 2**20
        ),
    )(tokens, scan_order, w_merge, bias, cotangent)
    results = (merged_out, token_grad, weight_grad, bias_grad)
    merged_out, token_grad, weight_grad, bias_grad = pl.pallas_call(
        hand_over,
        out_shape=tuple(jax.ShapeDtypeStruct(r.shape, r.dtype) for r in results),
        in_specs=[hbm] * 4,
        out_specs=(hbm,) * 4,
        scratch_shapes=[pltpu.VMEM(r.shape, r.dtype) for r in results] + [dma((8,))],
    )(*results)
    return merged_out, token_grad, weight_grad, bias_grad.reshape(do)


def solution(mesh):
    in_specs = (P("view", "span", None), P("view", None), P(), P(), P("view", "span", None))
    out_specs = (P("view", "span", None), P("view", "span", None), P(("view", "span"), None), P())
    return jax.shard_map(
        functools.partial(body, mesh.shape["view"], mesh.shape["span"]),
        mesh=mesh,
        in_specs=in_specs,
        out_specs=out_specs,
        check_vma=False,
    )
```

```python
import functools
import math

import jax
import jax.numpy as jnp
from jax import lax
from jax.experimental import pallas as pl
from jax.experimental.pallas import tpu as pltpu
from jax.sharding import PartitionSpec as P

MESH = pl.DeviceIdType.MESH
F32 = jnp.float32
BF16 = jnp.bfloat16
NN = (((1,), (0,)), ((), ()))
NT = (((1,), (1,)), ((), ()))
TN = (((0,), (0,)), ((), ()))


def dot(a, b, dims=NN):
    return lax.dot_general(a, b, dims, preferred_element_type=F32)


def one_hot(hit):
    return jnp.where(hit, 1.0, 0.0).astype(BF16)


def kernel(
    views,
    spans,
    cols,
    scale,
    tokens_hbm,
    order_hbm,
    w_hbm,
    bias_hbm,
    cot_hbm,
    merged_out_hbm,
    token_grad_hbm,
    weight_grad_hbm,
    bias_grad_hbm,
    merged_out_ref,
    token_grad_ref,
    weight_grad_ref,
    bias_grad_ref,
    w_ref,
    tokens_ref,
    order_ref,
    bias_ref,
    out_ref,
    recv_ref,
    back_ref,
    ret_ref,
    pick_ref,
    place_ref,
    rank_ref,
    code_ref,
    merged_ref,
    grad_ref,
    blocks_ref,
    cot_all,
    prod_a,
    prod_b,
    in_a,
    in_b,
    part_a,
    part_b,
    last_a,
    last_b,
    span_bias,
    in_sem,
    tok_send,
    tok_recv,
    back_send,
    back_recv,
    blk_send,
    blk_recv,
    ring_send,
    ring_recv,
    share_send,
    share_recv,
    bias_send,
    bias_recv,
    sum_a_send,
    sum_a_recv,
    sum_b_send,
    sum_b_recv,
    last_a_send,
    last_a_recv,
    last_b_send,
    last_b_recv,
):
    v = lax.axis_index("view")
    s = lax.axis_index("span")
    core = lax.rem(v, 2)
    z = v // 2
    nz = views // 2
    steps = nz // 2
    side = 4
    x, y = s // side, lax.rem(s, side)
    mine_half = x // 2
    tok, dm = tokens_ref.shape
    half = dm // 2
    mt = tok // 4
    cap = 3 * (tok // spans) // 2
    slot = 2 * cap
    lanes = blocks_ref.shape[3]
    width = 2 * lanes
    na = prod_a.shape[4]

    order_in = pltpu.make_async_copy(order_hbm, order_ref, in_sem.at[0])
    tokens_in = pltpu.make_async_copy(tokens_hbm.at[0], tokens_ref, in_sem.at[1])
    cot_in = pltpu.make_async_copy(cot_hbm.at[0], cot_all.at[z, core], in_sem.at[2])
    w_in = pltpu.make_async_copy(w_hbm, w_ref, in_sem.at[3])
    bias_in = pltpu.make_async_copy(bias_hbm, bias_ref, in_sem.at[4])
    merged_put = pltpu.make_async_copy(merged_out_ref, merged_out_hbm, in_sem.at[5])
    tokens_put = pltpu.make_async_copy(token_grad_ref, token_grad_hbm, in_sem.at[6])
    weight_put = pltpu.make_async_copy(weight_grad_ref, weight_grad_hbm, in_sem.at[7])
    bias_put = pltpu.make_async_copy(bias_grad_ref, bias_grad_hbm, in_sem.at[8])
    order_in.start()
    tokens_in.start()
    cot_in.start()

    barrier = pltpu.get_barrier_semaphore()

    @pl.loop(1, spans)
    def _(i):
        pl.semaphore_signal(barrier, inc=1, device_id=(v, s ^ i), device_id_type=MESH)

    @pl.loop(1, views)
    def _(i):
        pl.semaphore_signal(barrier, inc=1, device_id=(v ^ i, s), device_id_type=MESH)

    w_in.start()
    bias_in.start()

    def remote(src, dst, send, recv, device):
        return pltpu.make_async_remote_copy(
            src_ref=src,
            dst_ref=dst,
            send_sem=send,
            recv_sem=recv,
            device_id=device,
            device_id_type=MESH,
        )

    def tok_copy(h, i):
        at = h * spans + i
        return remote(
            out_ref.at[h, s ^ i], recv_ref.at[h, s], tok_send.at[at], tok_recv.at[at], (v, s ^ i)
        )

    def back_copy(i):
        return remote(
            back_ref.at[s ^ i], ret_ref.at[s], back_send.at[i], back_recv.at[i], (v, s ^ i)
        )

    def blk_copy(h, i):
        d = v ^ i
        at = h * views + i
        src = merged_ref.at[:, pl.ds(pl.multiple_of(d * width + h * lanes, lanes), lanes)]
        return remote(src, blocks_ref.at[h, v], blk_send.at[at], blk_recv.at[at], (d, s))

    def near(k):
        return lax.rem(z + 2 * nz - k, nz)

    def ring_copy(way, k):
        held = near(k - 1) if way == 0 else near(1 - k)
        to = near(-1) if way == 0 else near(1)
        ref = cot_all.at[held, core]
        if k == steps:
            ref = ref.at[:, way * half : (way + 1) * half]
        at = way * (steps + 1) + k
        return remote(ref, ref, ring_send.at[at], ring_recv.at[at], (to * 2 + core, s))

    def share_copy(k):
        ref = cot_all.at[near(k), core]
        return remote(ref, ref, share_send.at[k], share_recv.at[k], (v ^ 1, s))

    def bias_copy(i):
        ref = span_bias.at[s]
        return remote(ref, ref, bias_send.at[i], bias_recv.at[i], (v, s ^ i))

    def sum_a(h, i):
        at = h * side + i
        return remote(
            prod_a.at[h, :, y ^ i], in_a.at[h, y], sum_a_send.at[at], sum_a_recv.at[at], (v, s ^ i)
        )

    def sum_b(h, t, k):
        to = (2 * h + t) * side + y
        return remote(
            prod_b.at[h, t], in_b.at[k], sum_b_send.at[2 * h + t], sum_b_recv.at[k], (v, to)
        )

    def last_a_copy(h, t, k):
        to = (2 * h + t) * side + y
        return remote(
            part_a.at[h, t], last_a.at[k], last_a_send.at[2 * h + t], last_a_recv.at[k], (v, to)
        )

    def last_b_copy(i):
        return remote(
            part_b.at[y ^ i], last_b.at[y], last_b_send.at[i], last_b_recv.at[i], (v, s ^ i)
        )

    def pair_up(rows):
        n = rows.shape[1] // 2
        a = rows[:, :n].reshape(spans, cap, n)
        b = rows[:, n:].reshape(spans, cap, n)
        return jnp.concatenate([a, b], axis=1).astype(BF16)

    def unpair(slots):
        wide = slots.astype(F32)
        n = wide.shape[2]
        a = wide[:, :cap].reshape(spans * cap, n)
        b = wide[:, cap:].reshape(spans * cap, n)
        return jnp.concatenate([a, b], axis=1).astype(BF16)

    before = one_hot(
        lax.broadcasted_iota(jnp.int32, (tok, tok), 0)
        < lax.broadcasted_iota(jnp.int32, (tok, tok), 1)
    )
    bits = int(math.log2(tok))
    order_in.wait()
    mine = order_ref[0:1, pl.ds(pl.multiple_of(s * tok, tok), tok)]
    owner = lax.shift_right_logical(mine, bits)
    hot = jnp.where(lax.broadcasted_iota(jnp.int32, (spans, tok), 0) == owner, 1.0, 0.0)
    rank = jnp.sum(dot(hot.astype(BF16), before) * hot, axis=0, keepdims=True).astype(jnp.int32)
    to_slot = owner * cap + rank
    pick_ref[...] = one_hot(lax.broadcasted_iota(jnp.int32, (spans * cap, tok), 0) == to_slot)
    tokens_in.wait()

    def pieces(h):
        return [c + h * lanes for c in range(0, dm, width)]

    def fill(h):
        part = jnp.concatenate([tokens_ref[:, c : c + lanes] for c in pieces(h)], axis=1)
        out_ref[h] = pair_up(dot(pick_ref[...], part))
        recv_ref[h, s] = out_ref[h, s]

    fill(0)
    cot_in.wait()
    pl.semaphore_wait(barrier, spans + views - 2)
    ring_copy(0, 1).start()
    ring_copy(1, 1).start()

    @pl.loop(1, spans)
    def _(i):
        tok_copy(0, i).start()

    share_copy(0).start()
    fill(1)

    @pl.loop(1, spans)
    def _(i):
        tok_copy(1, i).start()

    order = jnp.concatenate([order_ref[0:1, c * tok : (c + 1) * tok] for c in range(spans)], axis=0)
    arriving = lax.shift_right_logical(order, bits) == s
    arrive = jnp.where(arriving, 1.0, 0.0)
    rank_in = dot(arrive.astype(BF16), before)
    rank_ref[...] = jnp.where(arriving, rank_in, -1.0)
    local = lax.rem(order, tok)
    col = lax.rem(local, cols)
    quadrant = (local // cols) * 2 + lax.rem(col, 2)
    code_ref[...] = jnp.where(arriving, quadrant * mt + col // 2 + 1, 0).astype(F32)

    @pl.loop(0, spans // 2)
    def _(t):
        k = lax.broadcasted_iota(jnp.int32, (cap, tok), 0).astype(F32)
        lane = lax.broadcasted_iota(jnp.int32, (cap, tok), 1).astype(F32) + 1.0
        found = []
        for c in range(2):
            rk = rank_ref[pl.ds(2 * t + c, 1), :]
            cd = code_ref[pl.ds(2 * t + c, 1), :]
            to = jnp.sum(jnp.where(rk == k, cd, 0.0), axis=1, keepdims=True)
            found.append(jnp.where(to == lane, 1.0, 0.0))
        place_ref[pl.ds(pl.multiple_of(t * slot, slot), slot), :] = jnp.concatenate(
            found, axis=0
        ).astype(BF16)

    def ring_step(k):
        ring_copy(0, k).wait_recv()
        ring_copy(1, k).wait_recv()
        if k < steps:
            ring_copy(0, k + 1).start()
            ring_copy(1, k + 1).start()
        share_copy(k).start()
        if k < steps:
            share_copy(nz - k).start()

    ring_step(1)
    w_in.wait()

    @pl.loop(0, 4)
    def _(q):
        w_rows = w_ref[pl.ds(pl.multiple_of(q * dm, dm), dm), :]
        g = dot(cot_all[z, core], w_rows, NT).astype(BF16)
        grad_ref[pl.ds(pl.multiple_of(q * mt, mt), mt), :] = g

    back_ref[...] = pair_up(dot(place_ref[...], grad_ref[...]))
    ret_ref[s] = back_ref[s]

    @pl.loop(1, spans)
    def _(i):
        back_copy(i).start()

    ring_step(2)

    def settle(h):
        @pl.loop(1, spans)
        def _(i):
            tok_copy(h, i).wait_recv()

        block = dot(place_ref[...], unpair(recv_ref[h]), TN).astype(BF16)
        for q in range(4):
            for n, c in enumerate(pieces(h)):
                merged_ref[:, q * dm + c : q * dm + c + lanes] = block[
                    q * mt : (q + 1) * mt, n * lanes : (n + 1) * lanes
                ]
        at = pl.ds(pl.multiple_of(v * width + h * lanes, lanes), lanes)
        blocks_ref[h, v] = merged_ref[:, at]

        @pl.loop(1, views)
        def _(i):
            blk_copy(h, i).start()

    settle(0)
    ring_step(3)
    settle(1)

    ring_step(4)

    @pl.loop(0, nz)
    def _(k):
        share_copy(k).wait_recv()

    depth = views * mt

    def multiply(h):
        @pl.loop(1, views)
        def _(i):
            blk_copy(h, i).wait_recv()

        lhs = blocks_ref[h].reshape(depth, lanes)
        prod_a[h] = dot(lhs, cot_all[:, :, :, :na].reshape(depth, na), TN).reshape(
            prod_a.shape[1:]
        )

        @pl.loop(1, side)
        def _(i):
            sum_a(h, i).start()

        prod_b[h] = dot(lhs, cot_all[:, :, :, na:].reshape(depth, dm - na), TN).reshape(
            prod_b.shape[1:]
        )
        for t in range(2):

            @pl.when(x != 2 * h + t)
            def _():
                sum_b(h, t, x).start()

            @pl.when(x == 2 * h + t)
            def _():
                in_b[x] = prod_b[h, t]

        in_a[h, y] = prod_a[h, :, y]

    def combine(h):
        @pl.loop(1, side)
        def _(i):
            sum_a(h, i).wait_recv()

        part_a[h] = jnp.sum(in_a[h], axis=0)
        for t in range(2):

            @pl.when(x != 2 * h + t)
            def _():
                last_a_copy(h, t, x).start()

            @pl.when(x == 2 * h + t)
            def _():
                last_a[x] = part_a[h, t]

        @pl.when(mine_half == h)
        def _():
            @pl.loop(1, side)
            def _(i):
                sum_b(h, 0, x ^ i).wait_recv()

            part_b[...] = jnp.sum(in_b[...], axis=0)
            last_b[y] = part_b[y]

            @pl.loop(1, side)
            def _(i):
                last_b_copy(i).start()

    multiply(0)
    multiply(1)

    bias_in.wait()

    @pl.loop(0, 4)
    def _(t):
        at = pl.ds(pl.multiple_of(t * 256, 256), 256)
        o = dot(merged_ref[...], w_ref[:, at]) + bias_ref[at].astype(F32)[None, :]
        merged_out_ref[0, :, at] = o.astype(BF16)

    merged_put.start()

    sums = dot(jnp.ones((8, depth), BF16), cot_all[...].reshape(depth, dm))
    for i in range(dm // 128):
        span_bias[s, i : i + 1, :] = sums[0:1, i * 128 : (i + 1) * 128]

    @pl.loop(1, spans)
    def _(i):
        bias_copy(i).start()

    @pl.loop(1, spans)
    def _(i):
        tok_copy(0, i).wait_send()
        tok_copy(1, i).wait_send()
        back_copy(i).wait_send()

    @pl.loop(1, views)
    def _(i):
        blk_copy(0, i).wait_send()
        blk_copy(1, i).wait_send()

    for k in range(1, steps + 1):
        ring_copy(0, k).wait_send()
        ring_copy(1, k).wait_send()

    @pl.loop(0, nz)
    def _(k):
        share_copy(k).wait_send()

    @pl.loop(1, spans)
    def _(i):
        back_copy(i).wait_recv()

    token_grad_ref[0] = dot(pick_ref[...], unpair(ret_ref[...]), TN).astype(BF16)
    tokens_put.start()

    combine(0)
    combine(1)

    @pl.loop(1, spans)
    def _(i):
        bias_copy(i).wait_recv()

    bias_grad_ref[...] = jnp.sum(span_bias[...], axis=0) * scale
    bias_put.start()

    @pl.loop(1, spans)
    def _(i):
        bias_copy(i).wait_send()

    @pl.loop(1, side)
    def _(i):
        sum_a(0, i).wait_send()
        sum_a(1, i).wait_send()

    @pl.loop(1, side)
    def _(i):
        last_a_copy(0, 0, x ^ i).wait_recv()
        last_b_copy(i).wait_recv()

    weight_grad_ref[:, :na] = jnp.sum(last_a[...], axis=0) * scale
    weight_grad_ref[:, na:] = jnp.sum(last_b[...], axis=0) * scale
    weight_put.start()

    @pl.loop(1, side)
    def _(i):
        last_b_copy(i).wait_send()

    for h in range(2):
        for t in range(2):

            @pl.when(x != 2 * h + t)
            def _():
                sum_b(h, t, x).wait_send()
                last_a_copy(h, t, x).wait_send()

    merged_put.wait()
    tokens_put.wait()
    bias_put.wait()
    weight_put.wait()


def hand_over(*refs):
    n = (len(refs) - 1) // 3
    sems = refs[-1]
    ins = [pltpu.make_async_copy(refs[i], refs[2 * n + i], sems.at[i]) for i in range(n)]
    outs = [pltpu.make_async_copy(refs[2 * n + i], refs[n + i], sems.at[n + i]) for i in range(n)]
    for copy in ins:
        copy.start()
    for read, write in zip(ins, outs):
        read.wait()
        write.start()
    for copy in outs:
        copy.wait()


def body(views, spans, tokens, scan_order, w_merge, bias, cotangent):
    tok, dm = tokens.shape[1:]
    merge_in, do = w_merge.shape
    mt = tok // 4
    half = dm // 2
    cap = 3 * (tok // spans) // 2
    slot = 2 * cap
    lanes = merge_in // views // 2
    part = merge_in // (views * spans)
    side = 4
    nz = views // 2
    na = 5 * do // 8
    nb = do - na
    scale = 1.0 / math.sqrt(views * spans * mt)
    hbm = pl.BlockSpec(memory_space=pl.ANY)
    dma = pltpu.SemaphoreType.DMA
    merged_out, token_grad, weight_grad, bias_grad = pl.pallas_call(
        functools.partial(kernel, views, spans, 128, scale),
        out_shape=(
            jax.ShapeDtypeStruct((1, mt, do), BF16),
            jax.ShapeDtypeStruct((1, tok, dm), BF16),
            jax.ShapeDtypeStruct((part, do), F32),
            jax.ShapeDtypeStruct((do // 128, 128), F32),
        ),
        in_specs=[hbm] * 5,
        out_specs=(hbm,) * 4,
        scratch_shapes=[
            pltpu.VMEM((1, mt, do), BF16),
            pltpu.VMEM((1, tok, dm), BF16),
            pltpu.VMEM((part, do), F32),
            pltpu.VMEM((do // 128, 128), F32),
            pltpu.VMEM((merge_in, do), BF16),
            pltpu.VMEM((tok, dm), BF16),
            pltpu.VMEM((1, spans * tok), jnp.int32),
            pltpu.VMEM((do,), BF16),
            pltpu.VMEM((2, spans, slot, half // 2), BF16),
            pltpu.VMEM((2, spans, slot, half // 2), BF16),
            pltpu.VMEM((spans, slot, half), BF16),
            pltpu.VMEM((spans, slot, half), BF16),
            pltpu.VMEM((spans * cap, tok), BF16),
            pltpu.VMEM((spans * cap, tok), BF16),
            pltpu.VMEM((spans, tok), F32),
            pltpu.VMEM((spans, tok), F32),
            pltpu.VMEM((mt, merge_in), BF16),
            pltpu.VMEM((tok, dm), BF16),
            pltpu.VMEM((2, views, mt, lanes), BF16),
            pltpu.VMEM((nz, 2, mt, do), BF16),
            pltpu.VMEM((2, 2, side, part, na), F32),
            pltpu.VMEM((2, 2, side, part, nb), F32),
            pltpu.VMEM((2, side, 2, part, na), F32),
            pltpu.VMEM((side, side, part, nb), F32),
            pltpu.VMEM((2, 2, part, na), F32),
            pltpu.VMEM((side, part, nb), F32),
            pltpu.VMEM((side, part, na), F32),
            pltpu.VMEM((side, part, nb), F32),
            pltpu.VMEM((spans, do // 128, 128), F32),
            dma((9,)),
            dma((2 * spans,)),
            dma((2 * spans,)),
            dma((spans,)),
            dma((spans,)),
            dma((2 * views,)),
            dma((2 * views,)),
            dma((nz + 2,)),
            dma((nz + 2,)),
            dma((nz,)),
            dma((nz,)),
            dma((spans,)),
            dma((spans,)),
            dma((2 * side,)),
            dma((2 * side,)),
            dma((side,)),
            dma((side,)),
            dma((side,)),
            dma((side,)),
            dma((side,)),
            dma((side,)),
        ],
        compiler_params=pltpu.CompilerParams(
            collective_id=0, has_side_effects=True, vmem_limit_bytes=60 * 2**20
        ),
    )(tokens, scan_order, w_merge, bias, cotangent)
    results = (merged_out, token_grad, weight_grad, bias_grad)
    merged_out, token_grad, weight_grad, bias_grad = pl.pallas_call(
        hand_over,
        out_shape=tuple(jax.ShapeDtypeStruct(r.shape, r.dtype) for r in results),
        in_specs=[hbm] * 4,
        out_specs=(hbm,) * 4,
        scratch_shapes=[pltpu.VMEM(r.shape, r.dtype) for r in results] + [dma((8,))],
    )(*results)
    return merged_out, token_grad, weight_grad, bias_grad.reshape(do)


def solution(mesh):
    in_specs = (P("view", "span", None), P("view", None), P(), P(), P("view", "span", None))
    out_specs = (P("view", "span", None), P("view", "span", None), P(("view", "span"), None), P())
    return jax.shard_map(
        functools.partial(body, mesh.shape["view"], mesh.shape["span"]),
        mesh=mesh,
        in_specs=in_specs,
        out_specs=out_specs,
        check_vma=False,
    )
```
